512 devices in a mesh: expert: 64 (over z, y), tensor: 8 (over x, core).
Axes of the slice: x: 4, y: 4, z: 16, core: 2. Of those that a mesh axis runs over, the one named last changes fastest.
Arguments:
- tokens: bfloat16 [24576, 2048], P(('expert', 'tensor')), may hold values from -400 to 400
- modulation: float32 [64, 3, 2048], P('expert'), may hold values from -4 to 4
- w_router: bfloat16 [2048, 64], replicated, may hold values from -0.125 to 0.125
- gate_weight: bfloat16 [64, 2048, 2048], P('expert', None, 'tensor'), may hold values from -0.125 to 0.125
- up_weight: bfloat16 [64, 2048, 2048], P('expert', None, 'tensor'), may hold values from -0.125 to 0.125
- down_weight: bfloat16 [64, 2048, 2048], P('expert', 'tensor'), may hold values from -0.125 to 0.125
- expert_ids: int32 [24576, 2], P(('expert', 'tensor')), may hold values from 0 to 63, all different within a row; in each aligned block of 384 rows (0 to 383, 384 to 767, ...) at most 16 rows name the same one
Outputs:
- branch_out: bfloat16 [24576, 2048], P(('expert', 'tensor'))
The draws below stay inside these ranges and needn't reach their ends.
Inputs may be any that keep to these rules, and one draw needn't show every extreme that they name: `expert_ids`: among the 384 rows of one image, no expert is named by more than 16 rows.
All inputs are finite; a program needn't handle non-finite values.
Results may differ from the reference program's by a relative error of at most 0.02.
Values may be sent and summed in bfloat16 or wider, within the bound.
No kernel may reach another device: no remote copies, remote signals or barrier semaphores. Data moves between devices by JAX's collectives and lax.ppermute only.
A program may use at most 64 MiB of HBM per device.

```python
import math
import jax
import jax.numpy as jnp
import numpy as np
from jax import lax

D = 2048
FF = 2048
TOP = 2
TOK_DEV = 48
EXPERTS = 64
IMAGES = 64
TOKENS = 24576
SLOT = 16
N_EXPERT = 64
N_TENSOR = 8


def draw_tokens(key, part):
    key = jax.random.fold_in(key, 11)
    key_base, key_rows, key_cols = jax.random.split(key, 3)
    row_scale = jnp.exp(jax.random.uniform(key_rows, (TOKENS, 1), jnp.float32, 0.0, math.log(10.0)))
    col_scale = jnp.exp(jax.random.uniform(key_cols, (1, D), jnp.float32, 0.0, math.log(10.0)))
    base = jnp.clip(jax.random.normal(key_base, (TOKENS, D), jnp.float32), -4.0, 4.0)
    values = base * row_scale * col_scale
    return jnp.clip(values, -400.0, 400.0).astype(jnp.bfloat16)


def block_scale(key, dims, cuts, low, largest):
    def one(axis_at, shards_of):
        steps = jax.random.uniform(jax.random.fold_in(jax.random.fold_in(key, 6), axis_at), (shards_of,), jnp.float32, low / len(cuts), largest / len(cuts))
        return jnp.repeat(jnp.exp(steps), dims[axis_at] // shards_of).reshape((-1,) + (1,) * (len(dims) - axis_at - 1))

    gain = one(*cuts[0])
    for cut in cuts[1:]:
        gain = gain * one(*cut)
    return gain


def routed_block(own_key, own, number, rows, amount, top, bound, slope):
    sequence = jax.random.permutation(own_key, amount)
    heavy_load, usual = load_shares(amount, rows * top, bound, slope, True), load_shares(amount, rows * top, bound, slope, False)
    places = jnp.arange(amount)

    def named(sizes, turn):
        used = int((sizes > 0).sum())
        fixed = max(1, used // 4)
        moved = fixed + (places - fixed + turn * (used - fixed)) % max(1, amount - fixed)
        return jnp.zeros((amount,), jnp.int32).at[sequence[jnp.where(places < fixed, places, moved)]].set(jnp.asarray(sizes, jnp.int32))

    sizes = jnp.where(number % 4 == 0, named(heavy_load, number // 4), named(usual, number - number // 4 - 1))
    mixed = jax.random.permutation(jax.random.fold_in(own, 3), amount)
    source_of, taker = mixed[0:amount // 2 * 2:2], mixed[1:amount // 2 * 2:2]
    room = jnp.minimum(sizes[source_of] - 1, bound - sizes[taker]) // 2
    room = jnp.where((source_of == sequence[0]) | (taker == sequence[0]) | (sizes[taker] == 0), 0, jnp.maximum(room, 0))
    moved = jax.random.randint(jax.random.fold_in(own, 4), (amount // 2,), 0, 1 << 20) % (room + 1)
    sizes = sizes.at[source_of].add(-moved).at[taker].add(moved)
    labels = jnp.searchsorted(jnp.cumsum(sizes), jnp.arange(rows * top), side="right").astype(jnp.int32)
    listing = labels.reshape(top, rows).T
    listing = listing[jax.random.permutation(jax.random.fold_in(own, 1), rows)]
    turn = jax.random.randint(jax.random.fold_in(own, 2), (rows, 1), 0, top)
    return jnp.take_along_axis(listing, (jnp.arange(top)[None, :] + turn) % top, axis=1)


def load_shares(count, total, most, slope, full):
    loads = [(1 << 20) // math.isqrt(rank ** slope) + 1 for rank in range(1, count + 1)]
    largest = most if full else min(most, max(-(-total // count), total * loads[0] // sum(loads)))
    least = 1 if total - largest >= count - 1 else 0
    given, rest = [largest] + [least] * (count - 1), total - largest - least * (count - 1)
    while rest > 0:
        movable = [i for i in range(1, count) if given[i] < largest] or [i for i in range(1, count) if given[i] < most]
        whole, left = sum([loads[i] for i in movable]), rest
        for i in movable:
            extra = min(most - given[i], max(1, left * loads[i] // whole), rest)
            given[i] = given[i] + extra
            rest = rest - extra
    return np.array(given)


def noise(key, extent, deviation, most, cuts=(), held_as=jnp.bfloat16):
    gain = block_scale(key, extent, cuts, -0.22, 0.18) if cuts else 1.0
    result = jax.random.normal(key, extent, jnp.float32) * deviation * gain
    return jnp.minimum(jnp.maximum(result, -most), most).astype(held_as)


def setup_inputs(seed: int = 0) -> dict:
    arg_keys = jax.random.split(jax.random.key(seed), 8)
    tokens = draw_tokens(jax.random.fold_in(arg_keys[7], 71), 0)
    modulation = noise(arg_keys[1], (IMAGES, 3, D), 1.0, 4.0, ((0, 64),), jnp.float32)
    w_router = noise(arg_keys[2], (D, EXPERTS), D ** -0.5, 0.125)
    gate_weight = noise(arg_keys[3], (EXPERTS, D, FF), D ** -0.5, 0.125, ((0, 64), (2, 8)))
    up_weight = noise(arg_keys[4], (EXPERTS, D, FF), D ** -0.5, 0.125, ((0, 64), (2, 8)))
    down_weight = noise(arg_keys[5], (EXPERTS, FF, D), FF ** -0.5, 0.125, ((0, 64), (1, 8)))
    expert_ids_keys = jax.random.split(jax.random.fold_in(arg_keys[6], 1), TOKENS // (N_TENSOR * TOK_DEV))
    expert_ids_turns = jax.random.permutation(jax.random.fold_in(arg_keys[6], 3), TOKENS // (N_TENSOR * TOK_DEV))
    expert_ids = jax.vmap(lambda own, number: routed_block(jax.random.fold_in(arg_keys[6], 2), own, number, N_TENSOR * TOK_DEV, EXPERTS, TOP, SLOT, 2))(expert_ids_keys, expert_ids_turns).reshape((TOKENS, TOP))
    return {"tokens": tokens, "modulation": modulation, "w_router": w_router, "gate_weight": gate_weight, "up_weight": up_weight, "down_weight": down_weight, "expert_ids": expert_ids}


EPS = 1e-06

def modulate(tokens, modulation):
    group_rows = N_TENSOR * TOK_DEV
    values = tokens.astype(jnp.float32).reshape(N_EXPERT, group_rows, D)
    average = lax.optimization_barrier(jnp.mean(values, axis=-1, keepdims=True))
    centred = values - average
    spread = lax.optimization_barrier(jnp.mean(centred * centred, axis=-1, keepdims=True))
    normed = centred * lax.rsqrt(spread + EPS)
    scaled = normed * (1.0 + modulation[:, 1][:, None, :]) + modulation[:, 0][:, None, :]
    return scaled.astype(jnp.bfloat16)

def expert_forward(operands):
    arrived, w_gate, w_up, w_down = operands
    flat_rows = arrived.reshape(-1, D)
    gate_part = jnp.dot(flat_rows, w_gate, preferred_element_type=jnp.float32)
    up_part = jnp.dot(flat_rows, w_up, preferred_element_type=jnp.float32)
    hidden = (jax.nn.silu(gate_part) * up_part).astype(jnp.bfloat16)
    block_width = FF // N_TENSOR
    total = jnp.zeros((flat_rows.shape[0], D), jnp.float32)
    for member in range(N_TENSOR):
        piece = jnp.dot(hidden[:, member * block_width:(member + 1) * block_width], w_down[member * block_width:(member + 1) * block_width], preferred_element_type=jnp.float32).astype(jnp.bfloat16)
        piece = lax.optimization_barrier(piece)
        total = total + piece.astype(jnp.float32)
    return total

def reference(tokens, modulation, w_router, gate_weight, up_weight, down_weight, expert_ids):
    group_rows = N_TENSOR * TOK_DEV
    modulated = modulate(tokens, modulation)
    choices_all = expert_ids.reshape(N_EXPERT, group_rows, TOP)
    logits = jnp.einsum('egd,dx->egx', modulated.astype(jnp.float32), w_router.astype(jnp.float32))
    chance = jnp.take_along_axis(jax.nn.sigmoid(logits), choices_all, axis=-1)
    combine = chance / lax.optimization_barrier(jnp.sum(chance, axis=-1, keepdims=True))
    counts = lax.optimization_barrier(jnp.sum((choices_all[..., None] == jnp.arange(EXPERTS, dtype=jnp.int32)).astype(jnp.int32), axis=-2))
    before = jnp.cumsum(counts, axis=1) - counts
    position = jnp.take_along_axis(before, choices_all, axis=-1)
    flat_index = choices_all * SLOT + position
    token_index = jnp.repeat(jnp.arange(group_rows, dtype=jnp.int32), TOP)

    def fill_table(flat_group):
        return jnp.full((EXPERTS * SLOT,), group_rows, jnp.int32).at[flat_group.reshape(-1)].set(token_index)
    slot_table = jax.vmap(fill_table)(flat_index)

    def take_rows(rows_group, table_group):
        return jnp.take(rows_group, table_group, axis=0, mode='fill', fill_value=0)
    outgoing = jax.vmap(take_rows)(modulated, slot_table).reshape(N_EXPERT, EXPERTS, SLOT, D)
    by_expert = jnp.transpose(outgoing, (1, 0, 2, 3))
    results = lax.map(expert_forward, (by_expert, gate_weight, up_weight, down_weight))
    results = results.reshape(EXPERTS, N_EXPERT, SLOT, D)
    image_index = jnp.arange(N_EXPERT, dtype=jnp.int32)[:, None, None]
    picked = results[choices_all, image_index, position]
    mixture = lax.optimization_barrier(jnp.sum(combine[..., None] * picked, axis=2))
    branch_out = (modulation[:, 2][:, None, :] * mixture).astype(jnp.bfloat16)
    return branch_out.reshape(TOKENS, D)
```

```python
import functools

import jax
import jax.numpy as jnp
from jax import lax
from jax.experimental import pallas as pl
from jax.experimental.pallas import tpu as pltpu
from jax.sharding import Mesh, PartitionSpec as P

EPS = 1e-06
F32 = jnp.float32
BF16 = jnp.bfloat16
CORES = 2
SLOT = 16
PAD = 64
ROUTE = 16
VMEM_LIMIT = 48 * 1024 * 1024


def call(kernel, out_shape, flops, nbytes):
    return pl.pallas_call(
        kernel,
        out_shape=out_shape,
        compiler_params=pltpu.CompilerParams(vmem_limit_bytes=VMEM_LIMIT),
        cost_estimate=pl.CostEstimate(flops=flops, bytes_accessed=nbytes, transcendentals=0),
    )


def high_low(value):
    high = value.astype(BF16).astype(F32)
    return high, value - high


def modulate_kernel(member_ref, tokens_ref, modulation_ref, router_ref, ids_ref, packet_ref):
    rows, width = tokens_ref.shape
    lanes = packet_ref.shape[2]
    values = tokens_ref[...].astype(F32)
    average = jnp.mean(values, axis=-1, keepdims=True)
    centred = values - average
    spread = jnp.mean(centred * centred, axis=-1, keepdims=True)
    normed = centred * lax.rsqrt(spread + EPS)
    modulated = (normed * (1.0 + modulation_ref[1]) + modulation_ref[0]).astype(BF16)
    logits = lax.dot_general(
        router_ref[...], modulated, (((1,), (1,)), ((), ())), preferred_element_type=F32
    )
    chance_all = jax.nn.sigmoid(logits)
    expert = lax.broadcasted_iota(jnp.int32, logits.shape, 0)
    ids = ids_ref[...]
    chance = [
        jnp.sum(jnp.where(expert == ids[c : c + 1], chance_all, 0.0), axis=0, keepdims=True)
        for c in range(2)
    ]
    total = chance[0] + chance[1]
    first_high, first_low = high_low(chance[0] / total)
    second_high, second_low = high_low(chance[1] / total)
    named = ids.astype(F32)
    route = jnp.concatenate(
        [
            named[0:1] + 1.0,
            named[1:2] + 1.0,
            first_high,
            first_low,
            second_high,
            second_low,
            jnp.zeros((ROUTE - 6, rows), F32),
        ],
        axis=0,
    ).astype(BF16)
    token = lax.broadcasted_iota(jnp.int32, (rows, lanes), 0)
    lane = lax.broadcasted_iota(jnp.int32, (rows, lanes), 1)
    place = jnp.where(lane == token + member_ref[0] * PAD, 1.0, 0.0).astype(BF16)
    placed = jnp.dot(route, place, preferred_element_type=F32).astype(BF16)
    for member in range(packet_ref.shape[0]):
        quarter = member // CORES
        packet_ref[member, 0:rows, :] = modulated[:, quarter * lanes : (quarter + 1) * lanes]
        packet_ref[member, rows:PAD, :] = placed


def fill_kernel(core_ref, packet_ref, slots_ref, route_ref):
    members, _, lanes = packet_ref.shape
    count = slots_ref.shape[0]
    half = SLOT // CORES
    experts = count // half
    tokens = PAD - ROUTE
    route = packet_ref[0, tokens:PAD, :].astype(F32)
    for member in range(1, members):
        route = route + packet_ref[member, tokens:PAD, :].astype(F32)
    everything = packet_ref.shape[0] * PAD
    named = [route[c : c + 1].astype(jnp.int32) - 1 for c in range(2)]
    expert = lax.broadcasted_iota(jnp.int32, (experts, everything), 0)
    names = [expert == named[c] for c in range(2)]
    either = jnp.where(names[0] | names[1], 1.0, 0.0).astype(BF16)
    earlier = lax.broadcasted_iota(jnp.int32, (everything, everything), 0) < (
        lax.broadcasted_iota(jnp.int32, (everything, everything), 1)
    )
    before = jnp.dot(
        either, jnp.where(earlier, 1.0, 0.0).astype(BF16), preferred_element_type=F32
    )
    place = []
    for c in range(2):
        position = jnp.sum(jnp.where(names[c], before, 0.0), axis=0, keepdims=True)
        position = position.astype(jnp.int32) - core_ref[0] * half
        here = (position >= 0) & (position < half) & (named[c] >= 0)
        place.append(jnp.where(here, named[c] * half + position, -1))
    slot = lax.broadcasted_iota(jnp.int32, (count, everything), 0)
    pick = jnp.where((slot == place[0]) | (slot == place[1]), 1.0, 0.0).astype(BF16)
    rows = packet_ref[...].reshape(everything, lanes)
    slots_ref[...] = jnp.dot(pick, rows, preferred_element_type=F32).astype(BF16)
    route_ref[...] = jnp.concatenate(
        [place[0].astype(F32), place[1].astype(F32), route[2:6], jnp.zeros((2, everything), F32)],
        axis=0,
    )


def expert_kernel(
    quarter_ref, a_ref, b_ref, c_ref, d_ref, g0, u0, w0, g1, u1, w1, out_ref
):
    width = a_ref.shape[1]
    blocks = out_ref.shape[0]
    hidden = []
    for gate_ref, up_ref in ((g0, u0), (g1, u1)):
        gate = up = None
        for step, ref in enumerate((a_ref, b_ref, c_ref, d_ref)):
            start = pl.multiple_of(lax.rem(quarter_ref[0] + step, blocks) * width, width)
            gate_term = jnp.dot(ref[...], gate_ref[pl.ds(start, width), :], preferred_element_type=F32)
            up_term = jnp.dot(ref[...], up_ref[pl.ds(start, width), :], preferred_element_type=F32)
            gate = gate_term if gate is None else gate + gate_term
            up = up_term if up is None else up + up_term
        hidden.append((gate * jax.nn.sigmoid(gate) * up).astype(BF16))
    for block in range(blocks):
        cols = slice(block * width, (block + 1) * width)
        out_ref[block] = (
            jnp.dot(hidden[0], w0[:, cols], preferred_element_type=F32)
            + jnp.dot(hidden[1], w1[:, cols], preferred_element_type=F32)
        ).astype(BF16)


def sum_kernel(parts_ref, out_ref):
    total = parts_ref[0].astype(F32)
    for part in range(1, parts_ref.shape[0]):
        total = total + parts_ref[part].astype(F32)
    out_ref[...] = total.astype(BF16)


def combine_kernel(slots_ref, route_ref, out_ref):
    count = slots_ref.shape[0]
    everything = route_ref.shape[1]
    slot = lax.broadcasted_iota(jnp.int32, (count, everything), 0)
    first = slot == route_ref[0:1].astype(jnp.int32)
    second = slot == route_ref[1:2].astype(jnp.int32)
    high = jnp.where(first, route_ref[2:3], 0.0) + jnp.where(second, route_ref[4:5], 0.0)
    low = jnp.where(first, route_ref[3:4], 0.0) + jnp.where(second, route_ref[5:6], 0.0)
    rows = slots_ref[...]
    dims = (((0,), (0,)), ((), ()))
    mixed = lax.dot_general(high.astype(BF16), rows, dims, preferred_element_type=F32)
    mixed = mixed + lax.dot_general(low.astype(BF16), rows, dims, preferred_element_type=F32)
    mixed = mixed.astype(BF16)
    tokens = out_ref.shape[1]
    for member in range(out_ref.shape[0]):
        out_ref[member] = mixed[member * PAD : member * PAD + tokens, :]


def gate_kernel(parts_ref, modulation_ref, out_ref):
    lanes = parts_ref.shape[2]
    for quarter in range(parts_ref.shape[0] // CORES):
        total = parts_ref[CORES * quarter].astype(F32)
        for core in range(1, CORES):
            total = total + parts_ref[CORES * quarter + core].astype(F32)
        cols = slice(quarter * lanes, (quarter + 1) * lanes)
        out_ref[:, cols] = (modulation_ref[2][:, cols] * total).astype(BF16)


def body(tokens, modulation, w_router, gate_weight, up_weight, down_weight, expert_ids):
    chips = lax.axis_size("x")
    members = chips * CORES
    own, width = tokens.shape
    lanes = width // chips
    experts = w_router.shape[1]
    images = lax.axis_size("expert")
    half = SLOT // CORES
    count = experts * half
    x = lax.axis_index("x")
    core = lax.axis_index("c")
    tensor = ("x", "c")
    modulation = jnp.transpose(modulation, (1, 0, 2))
    swap = [(0, 1), (1, 0)]
    weights = [gate_weight[0], up_weight[0], down_weight[0]]
    others = [lax.ppermute(w, "c", swap) for w in weights]

    packet = call(
        modulate_kernel,
        jax.ShapeDtypeStruct((members, PAD, lanes), BF16),
        2 * own * width * experts,
        4 * own * width,
    )(
        (x * CORES + core).astype(jnp.int32).reshape(1),
        tokens,
        modulation,
        w_router.T,
        expert_ids.T,
    )
    packet = lax.all_to_all(packet, tensor, 0, 0, tiled=True)
    slots, route = call(
        fill_kernel,
        (
            jax.ShapeDtypeStruct((count, lanes), BF16),
            jax.ShapeDtypeStruct((8, members * PAD), F32),
        ),
        2 * count * members * PAD * lanes,
        4 * count * lanes,
    )(core.astype(jnp.int32).reshape(1), packet)
    arrived = lax.all_to_all(
        slots.reshape(experts, half, lanes), "expert", 0, 0, tiled=True
    ).reshape(count, lanes)

    blocks = [arrived] + [
        lax.ppermute(arrived, "x", [(i, (i - step) % chips) for i in range(chips)])
        for step in range(1, chips)
    ]
    partial = call(
        expert_kernel,
        jax.ShapeDtypeStruct((chips, count, lanes), BF16),
        6 * count * width * gate_weight.shape[2] * CORES,
        12 * width * gate_weight.shape[2],
    )(x.astype(jnp.int32).reshape(1), *blocks, *weights, *others)
    partial = lax.all_to_all(partial, "x", 0, 0, tiled=True)
    summed = call(
        sum_kernel, jax.ShapeDtypeStruct((count, lanes), BF16), count * width, 2 * count * width
    )(partial)
    produced = lax.all_to_all(
        summed.reshape(images, half, lanes), "expert", 0, 0, tiled=True
    ).reshape(count, lanes)
    mixed = call(
        combine_kernel,
        jax.ShapeDtypeStruct((members, own, lanes), BF16),
        4 * count * members * PAD * lanes,
        4 * count * lanes,
    )(produced, route)
    mixed = lax.all_to_all(mixed, tensor, 0, 0, tiled=True)
    return call(
        gate_kernel, jax.ShapeDtypeStruct((own, width), BF16), own * width, 4 * own * width
    )(mixed, modulation)


def solution(mesh):
    images, members = mesh.devices.shape
    fine = Mesh(mesh.devices.reshape(images, members // CORES, CORES), ("expert", "x", "c"))
    tensor = ("x", "c")
    rows = P(("expert", "x", "c"), None)
    placed = (
        rows,
        P("expert", None, None),
        P(),
        P("expert", None, tensor),
        P("expert", None, tensor),
        P("expert", tensor, None),
        rows,
    )
    return jax.shard_map(body, mesh=fine, in_specs=placed, out_specs=rows, check_vma=False)
```

```python
import functools

import jax
import jax.numpy as jnp
from jax import lax
from jax.experimental import pallas as pl
from jax.experimental.pallas import tpu as pltpu
from jax.sharding import Mesh, PartitionSpec as P

EPS = 1e-06
F32 = jnp.float32
BF16 = jnp.bfloat16
CORES = 2
SLOT = 16
PAD = 64
ROUTE = 16
VMEM_LIMIT = 12 * 1024 * 1024


def call(kernel, out_shape, flops, nbytes):
    return pl.pallas_call(
        kernel,
        out_shape=out_shape,
        compiler_params=pltpu.CompilerParams(vmem_limit_bytes=VMEM_LIMIT),
        cost_estimate=pl.CostEstimate(flops=flops, bytes_accessed=nbytes, transcendentals=0),
    )


def high_low(value):
    high = value.astype(BF16).astype(F32)
    return high, value - high


def modulate_kernel(member_ref, tokens_ref, modulation_ref, router_ref, ids_ref, packet_ref):
    rows, width = tokens_ref.shape
    lanes = packet_ref.shape[2]
    values = tokens_ref[...].astype(F32)
    average = jnp.mean(values, axis=-1, keepdims=True)
    centred = values - average
    spread = jnp.mean(centred * centred, axis=-1, keepdims=True)
    normed = centred * lax.rsqrt(spread + EPS)
    modulated = (normed * (1.0 + modulation_ref[1]) + modulation_ref[0]).astype(BF16)
    logits = lax.dot_general(
        router_ref[...], modulated, (((1,), (1,)), ((), ())), preferred_element_type=F32
    )
    chance_all = jax.nn.sigmoid(logits)
    expert = lax.broadcasted_iota(jnp.int32, logits.shape, 0)
    ids = ids_ref[...]
    chance = [
        jnp.sum(jnp.where(expert == ids[c : c + 1], chance_all, 0.0), axis=0, keepdims=True)
        for c in range(2)
    ]
    total = chance[0] + chance[1]
    first_high, first_low = high_low(chance[0] / total)
    second_high, second_low = high_low(chance[1] / total)
    named = ids.astype(F32)
    route = jnp.concatenate(
        [
            named[0:1] + 1.0,
            named[1:2] + 1.0,
            first_high,
            first_low,
            second_high,
            second_low,
            jnp.zeros((ROUTE - 6, rows), F32),
        ],
        axis=0,
    ).astype(BF16)
    token = lax.broadcasted_iota(jnp.int32, (rows, lanes), 0)
    lane = lax.broadcasted_iota(jnp.int32, (rows, lanes), 1)
    place = jnp.where(lane == token + member_ref[0] * PAD, 1.0, 0.0).astype(BF16)
    placed = jnp.dot(route, place, preferred_element_type=F32).astype(BF16)
    for member in range(packet_ref.shape[0]):
        quarter = member // CORES
        packet_ref[member, 0:rows, :] = modulated[:, quarter * lanes : (quarter + 1) * lanes]
        packet_ref[member, rows:PAD, :] = placed


def fill_kernel(core_ref, packet_ref, slots_ref, route_ref):
    members, _, lanes = packet_ref.shape
    count = slots_ref.shape[0]
    half = SLOT // CORES
    experts = count // half
    tokens = PAD - ROUTE
    route = packet_ref[0, tokens:PAD, :].astype(F32)
    for member in range(1, members):
        route = route + packet_ref[member, tokens:PAD, :].astype(F32)
    everything = packet_ref.shape[0] * PAD
    named = [route[c : c + 1].astype(jnp.int32) - 1 for c in range(2)]
    expert = lax.broadcasted_iota(jnp.int32, (experts, everything), 0)
    names = [expert == named[c] for c in range(2)]
    either = jnp.where(names[0] | names[1], 1.0, 0.0).astype(BF16)
    earlier = lax.broadcasted_iota(jnp.int32, (everything, everything), 0) < (
        lax.broadcasted_iota(jnp.int32, (everything, everything), 1)
    )
    before = jnp.dot(
        either, jnp.where(earlier, 1.0, 0.0).astype(BF16), preferred_element_type=F32
    )
    place = []
    for c in range(2):
        position = jnp.sum(jnp.where(names[c], before, 0.0), axis=0, keepdims=True)
        position = position.astype(jnp.int32) - core_ref[0] * half
        here = (position >= 0) & (position < half) & (named[c] >= 0)
        place.append(jnp.where(here, named[c] * half + position, -1))
    slot = lax.broadcasted_iota(jnp.int32, (count, everything), 0)
    pick = jnp.where((slot == place[0]) | (slot == place[1]), 1.0, 0.0).astype(BF16)
    rows = packet_ref[...].reshape(everything, lanes)
    slots_ref[...] = jnp.dot(pick, rows, preferred_element_type=F32).astype(BF16)
    route_ref[...] = jnp.concatenate(
        [place[0].astype(F32), place[1].astype(F32), route[2:6], jnp.zeros((2, everything), F32)],
        axis=0,
    )


def cut(quarter_ref, step, blocks, width):
    return pl.ds(pl.multiple_of(lax.rem(quarter_ref[0] + step, blocks) * width, width), width)


def near_kernel(quarter_ref, a_ref, l_ref, r_ref, g0, u0, g1, u1, out_ref):
    width = a_ref.shape[1]
    blocks = g0.shape[0] // width
    for index, weight_ref in enumerate((g0, u0, g1, u1)):
        total = None
        for step, ref in ((0, a_ref), (1, r_ref), (blocks - 1, l_ref)):
            rows = weight_ref[cut(quarter_ref, step, blocks, width), :]
            term = jnp.dot(ref[...], rows, preferred_element_type=F32)
            total = term if total is None else total + term
        out_ref[index] = total


def far_kernel(
    quarter_ref, near_ref, top_ref, bottom_ref, g0, u0, g1, u1, w0, w1, hidden_ref, out_ref
):
    rows, width = top_ref.shape
    blocks = g0.shape[0] // width
    where = cut(quarter_ref, blocks // 2, blocks, width)
    for part, ref in enumerate((top_ref, bottom_ref)):
        span = slice(part * rows, (part + 1) * rows)
        total = [
            near_ref[index, span, :]
            + jnp.dot(ref[...], weight_ref[where, :], preferred_element_type=F32)
            for index, weight_ref in enumerate((g0, u0, g1, u1))
        ]
        far = None
        for core, down_ref in enumerate((w0, w1)):
            gate, up = total[2 * core], total[2 * core + 1]
            hidden = (gate * jax.nn.sigmoid(gate) * up).astype(BF16)
            hidden_ref[core, span, :] = hidden
            term = jnp.dot(hidden, down_ref[:, where], preferred_element_type=F32)
            far = term if far is None else far + term
        out_ref[part] = far.astype(BF16)


def down(hidden_ref, w0, w1, where):
    return jnp.dot(hidden_ref[0], w0[:, where], preferred_element_type=F32) + jnp.dot(
        hidden_ref[1], w1[:, where], preferred_element_type=F32
    )


def next_kernel(quarter_ref, hidden_ref, w0, w1, top_ref, bottom_ref, right_ref, left_ref):
    half, width = top_ref.shape
    blocks = w0.shape[1] // width
    right = down(hidden_ref, w0, w1, cut(quarter_ref, 1, blocks, width))
    right_ref[0:half, :] = (right[0:half] + top_ref[...].astype(F32)).astype(BF16)
    right_ref[half:, :] = right[half:].astype(BF16)
    left = down(hidden_ref, w0, w1, cut(quarter_ref, blocks - 1, blocks, width))
    left_ref[0:half, :] = left[0:half].astype(BF16)
    left_ref[half:, :] = (left[half:] + bottom_ref[...].astype(F32)).astype(BF16)


def own_kernel(quarter_ref, hidden_ref, w0, w1, out_ref):
    width = out_ref.shape[1]
    out_ref[...] = down(hidden_ref, w0, w1, cut(quarter_ref, 0, w0.shape[1] // width, width))


def sum_kernel(own_ref, left_ref, right_ref, out_ref):
    out_ref[...] = (
        own_ref[...] + left_ref[...].astype(F32) + right_ref[...].astype(F32)
    ).astype(BF16)


def combine_kernel(slots_ref, route_ref, out_ref):
    count = slots_ref.shape[0]
    everything = route_ref.shape[1]
    slot = lax.broadcasted_iota(jnp.int32, (count, everything), 0)
    first = slot == route_ref[0:1].astype(jnp.int32)
    second = slot == route_ref[1:2].astype(jnp.int32)
    high = jnp.where(first, route_ref[2:3], 0.0) + jnp.where(second, route_ref[4:5], 0.0)
    low = jnp.where(first, route_ref[3:4], 0.0) + jnp.where(second, route_ref[5:6], 0.0)
    rows = slots_ref[...]
    dims = (((0,), (0,)), ((), ()))
    mixed = lax.dot_general(high.astype(BF16), rows, dims, preferred_element_type=F32)
    mixed = mixed + lax.dot_general(low.astype(BF16), rows, dims, preferred_element_type=F32)
    mixed = mixed.astype(BF16)
    tokens = out_ref.shape[1]
    for member in range(out_ref.shape[0]):
        out_ref[member] = mixed[member * PAD : member * PAD + tokens, :]


def gate_kernel(parts_ref, modulation_ref, out_ref):
    lanes = parts_ref.shape[2]
    for quarter in range(parts_ref.shape[0] // CORES):
        total = parts_ref[CORES * quarter].astype(F32)
        for core in range(1, CORES):
            total = total + parts_ref[CORES * quarter + core].astype(F32)
        cols = slice(quarter * lanes, (quarter + 1) * lanes)
        out_ref[:, cols] = (modulation_ref[2][:, cols] * total).astype(BF16)


def body(tokens, modulation, w_router, gate_weight, up_weight, down_weight, expert_ids):
    chips = lax.axis_size("x")
    members = chips * CORES
    own, width = tokens.shape
    lanes = width // chips
    experts = w_router.shape[1]
    images = lax.axis_size("expert")
    half = SLOT // CORES
    count = experts * half
    x = lax.axis_index("x")
    core = lax.axis_index("c")
    tensor = ("x", "c")
    modulation = jnp.transpose(modulation, (1, 0, 2))
    swap = [(0, 1), (1, 0)]
    weights = [gate_weight[0], up_weight[0], down_weight[0]]
    others = [lax.ppermute(w, "c", swap) for w in weights]

    packet = call(
        modulate_kernel,
        jax.ShapeDtypeStruct((members, PAD, lanes), BF16),
        2 * own * width * experts,
        4 * own * width,
    )(
        (x * CORES + core).astype(jnp.int32).reshape(1),
        tokens,
        modulation,
        w_router.T,
        expert_ids.T,
    )
    packet = lax.all_to_all(packet, tensor, 0, 0, tiled=True)
    slots, route = call(
        fill_kernel,
        (
            jax.ShapeDtypeStruct((count, lanes), BF16),
            jax.ShapeDtypeStruct((8, members * PAD), F32),
        ),
        2 * count * members * PAD * lanes,
        4 * count * lanes,
    )(core.astype(jnp.int32).reshape(1), packet)
    arrived = lax.all_to_all(
        slots.reshape(experts, half, lanes), "expert", 0, 0, tiled=True
    ).reshape(count, lanes)

    quarter = x.astype(jnp.int32).reshape(1)
    onward = [(i, (i + 1) % chips) for i in range(chips)]
    backward = [(i, (i - 1) % chips) for i in range(chips)]
    g0, u0, w0 = weights
    g1, u1, w1 = others
    cols = gate_weight.shape[2]
    cut_rows = count // 2
    left = lax.ppermute(arrived, "x", onward)
    right = lax.ppermute(arrived, "x", backward)
    top = lax.ppermute(left[:cut_rows], "x", onward)
    bottom = lax.ppermute(right[cut_rows:], "x", backward)
    near = call(
        near_kernel,
        jax.ShapeDtypeStruct((4, count, cols), F32),
        24 * count * lanes * cols,
        16 * lanes * cols + 16 * count * cols,
    )(quarter, arrived, left, right, g0, u0, g1, u1)
    hidden, far = call(
        far_kernel,
        (
            jax.ShapeDtypeStruct((2, count, cols), BF16),
            jax.ShapeDtypeStruct((2, cut_rows, lanes), BF16),
        ),
        12 * count * lanes * cols,
        16 * count * cols,
    )(quarter, near, top, bottom, g0, u0, g1, u1, w0, w1)
    top = lax.ppermute(far[0], "x", onward)
    bottom = lax.ppermute(far[1], "x", backward)
    piece = jax.ShapeDtypeStruct((count, lanes), BF16)
    to_right, to_left = call(
        next_kernel, (piece, piece), 8 * count * lanes * cols, 8 * count * lanes
    )(quarter, hidden, w0, w1, top, bottom)
    left = lax.ppermute(to_right, "x", onward)
    right = lax.ppermute(to_left, "x", backward)
    own_sum = call(
        own_kernel,
        jax.ShapeDtypeStruct((count, lanes), F32),
        4 * count * lanes * cols,
        4 * count * lanes,
    )(quarter, hidden, w0, w1)
    summed = call(sum_kernel, piece, 2 * count * lanes, 10 * count * lanes)(
        own_sum, left, right
    )
    produced = lax.all_to_all(
        summed.reshape(images, half, lanes), "expert", 0, 0, tiled=True
    ).reshape(count, lanes)
    mixed = call(
        combine_kernel,
        jax.ShapeDtypeStruct((members, own, lanes), BF16),
        4 * count * members * PAD * lanes,
        4 * count * lanes,
    )(produced, route)
    mixed = lax.all_to_all(mixed, tensor, 0, 0, tiled=True)
    return call(
        gate_kernel, jax.ShapeDtypeStruct((own, width), BF16), own * width, 4 * own * width
    )(mixed, modulation)


def solution(mesh):
    images, members = mesh.devices.shape
    fine = Mesh(mesh.devices.reshape(images, members // CORES, CORES), ("expert", "x", "c"))
    tensor = ("x", "c")
    rows = P(("expert", "x", "c"), None)
    placed = (
        rows,
        P("expert", None, None),
        P(),
        P("expert", None, tensor),
        P("expert", None, tensor),
        P("expert", tensor, None),
        rows,
    )
    return jax.shard_map(body, mesh=fine, in_specs=placed, out_specs=rows, check_vma=False)
```

```python
import functools

import jax
import jax.numpy as jnp
from jax import lax
from jax.experimental import pallas as pl
from jax.experimental.pallas import tpu as pltpu
from jax.sharding import Mesh, PartitionSpec as P

EPS = 1e-06
F32 = jnp.float32
BF16 = jnp.bfloat16
CORES = 2
SLOT = 16
PAD = 64
ROUTE = 16
VMEM_LIMIT = 12 * 1024 * 1024
FIRST_LIMIT = 60 * 1024 * 1024


def call(kernel, out_shape, flops, nbytes, spaces=None, scratch=(), limit=VMEM_LIMIT):
    kinds = {"v": pltpu.VMEM, "h": pltpu.HBM}
    specs = {}
    if spaces is not None:
        specs = {"in_specs": [pl.BlockSpec(memory_space=kinds[kind]) for kind in spaces]}
    return pl.pallas_call(
        kernel,
        out_shape=out_shape,
        scratch_shapes=scratch,
        compiler_params=pltpu.CompilerParams(vmem_limit_bytes=limit),
        cost_estimate=pl.CostEstimate(flops=flops, bytes_accessed=nbytes, transcendentals=0),
        **specs,
    )


def high_low(value):
    high = value.astype(BF16).astype(F32)
    return high, value - high


def modulate_kernel(
    member_ref, ids_ref, tokens_in, modulation_in, router_in, packet_ref,
    tokens_ref, modulation_ref, router_ref, arrived,
):
    copies = [
        pltpu.make_async_copy(source, target, arrived.at[index])
        for index, (source, target) in enumerate(
            ((tokens_in, tokens_ref), (modulation_in, modulation_ref), (router_in, router_ref))
        )
    ]
    for copy in copies:
        copy.start()
    copies[0].wait()
    rows, width = tokens_ref.shape
    lanes = packet_ref.shape[2]
    values = tokens_ref[...].astype(F32)
    average = jnp.mean(values, axis=-1, keepdims=True)
    centred = values - average
    spread = jnp.mean(centred * centred, axis=-1, keepdims=True)
    normed = centred * lax.rsqrt(spread + EPS)
    copies[1].wait()
    copies[2].wait()
    modulated = (normed * (1.0 + modulation_ref[1]) + modulation_ref[0]).astype(BF16)
    logits = lax.dot_general(
        router_ref[...], modulated, (((1,), (1,)), ((), ())), preferred_element_type=F32
    )
    chance_all = jax.nn.sigmoid(logits)
    expert = lax.broadcasted_iota(jnp.int32, logits.shape, 0)
    ids = ids_ref[...]
    chance = [
        jnp.sum(jnp.where(expert == ids[c : c + 1], chance_all, 0.0), axis=0, keepdims=True)
        for c in range(2)
    ]
    total = chance[0] + chance[1]
    first_high, first_low = high_low(chance[0] / total)
    second_high, second_low = high_low(chance[1] / total)
    named = ids.astype(F32)
    route = jnp.concatenate(
        [
            named[0:1] + 1.0,
            named[1:2] + 1.0,
            first_high,
            first_low,
            second_high,
            second_low,
            jnp.zeros((ROUTE - 6, rows), F32),
        ],
        axis=0,
    ).astype(BF16)
    token = lax.broadcasted_iota(jnp.int32, (rows, lanes), 0)
    lane = lax.broadcasted_iota(jnp.int32, (rows, lanes), 1)
    place = jnp.where(lane == token + member_ref[0] * PAD, 1.0, 0.0).astype(BF16)
    placed = jnp.dot(route, place, preferred_element_type=F32).astype(BF16)
    for member in range(packet_ref.shape[0]):
        quarter = member // CORES
        packet_ref[member, 0:rows, :] = modulated[:, quarter * lanes : (quarter + 1) * lanes]
        packet_ref[member, rows:PAD, :] = placed


def fill_kernel(core_ref, packet_ref, slots_ref, route_ref):
    members, _, lanes = packet_ref.shape
    count = slots_ref.shape[0]
    half = SLOT // CORES
    experts = count // half
    tokens = PAD - ROUTE
    route = packet_ref[0, tokens:PAD, :].astype(F32)
    for member in range(1, members):
        route = route + packet_ref[member, tokens:PAD, :].astype(F32)
    everything = packet_ref.shape[0] * PAD
    named = [route[c : c + 1].astype(jnp.int32) - 1 for c in range(2)]
    expert = lax.broadcasted_iota(jnp.int32, (experts, everything), 0)
    names = [expert == named[c] for c in range(2)]
    either = jnp.where(names[0] | names[1], 1.0, 0.0).astype(BF16)
    earlier = lax.broadcasted_iota(jnp.int32, (everything, everything), 0) < (
        lax.broadcasted_iota(jnp.int32, (everything, everything), 1)
    )
    before = jnp.dot(
        either, jnp.where(earlier, 1.0, 0.0).astype(BF16), preferred_element_type=F32
    )
    place = []
    for c in range(2):
        position = jnp.sum(jnp.where(names[c], before, 0.0), axis=0, keepdims=True)
        position = position.astype(jnp.int32) - core_ref[0] * half
        here = (position >= 0) & (position < half) & (named[c] >= 0)
        place.append(jnp.where(here, named[c] * half + position, -1))
    slot = lax.broadcasted_iota(jnp.int32, (count, everything), 0)
    pick = jnp.where((slot == place[0]) | (slot == place[1]), 1.0, 0.0).astype(BF16)
    rows = packet_ref[...].reshape(everything, lanes)
    slots_ref[...] = jnp.dot(pick, rows, preferred_element_type=F32).astype(BF16)
    route_ref[...] = jnp.concatenate(
        [place[0].astype(F32), place[1].astype(F32), route[2:6], jnp.zeros((2, everything), F32)],
        axis=0,
    )


def cut(quarter_ref, step, blocks, width):
    return pl.ds(pl.multiple_of(lax.rem(quarter_ref[0] + step, blocks) * width, width), width)


def near_kernel(quarter_ref, a_ref, l0, l1, r0, r1, g0, u0, g1, u1, out_ref, held, arrived):
    rows, width = l0.shape
    blocks = g0.shape[0] // width
    copies = [
        [
            pltpu.make_async_copy(
                weight_ref.at[cut(quarter_ref, step, blocks, width), :],
                held.at[index, place],
                arrived.at[index, place],
            )
            for place, step in enumerate((0, blocks - 1, 1))
        ]
        for index, weight_ref in enumerate((g0, u0, g1, u1))
    ]
    for group in copies:
        for copy in group:
            copy.start()
    for index, group in enumerate(copies):
        for copy in group:
            copy.wait()
        for part, (l_ref, r_ref) in enumerate(((l0, r0), (l1, r1))):
            span = slice(part * rows, (part + 1) * rows)
            out_ref[index, span, :] = (
                jnp.dot(a_ref[span, :], held[index, 0], preferred_element_type=F32)
                + jnp.dot(l_ref[...], held[index, 1], preferred_element_type=F32)
                + jnp.dot(r_ref[...], held[index, 2], preferred_element_type=F32)
            )


def far_kernel(
    quarter_ref, near_ref, top_ref, bottom_ref, g0, u0, g1, u1, w0, w1,
    hidden_ref, out_ref, held, held_down, arrived,
):
    rows, width = top_ref.shape
    blocks = g0.shape[0] // width
    where = cut(quarter_ref, blocks // 2, blocks, width)
    copies = [
        pltpu.make_async_copy(weight_ref.at[where, :], held.at[index], arrived.at[index])
        for index, weight_ref in enumerate((g0, u0, g1, u1))
    ] + [
        pltpu.make_async_copy(down_ref.at[:, where], held_down.at[core], arrived.at[4 + core])
        for core, down_ref in enumerate((w0, w1))
    ]
    for copy in copies:
        copy.start()
    for core in range(2):
        copies[2 * core].wait()
        copies[2 * core + 1].wait()
        for part, ref in enumerate((top_ref, bottom_ref)):
            span = slice(part * rows, (part + 1) * rows)
            gate, up = [
                near_ref[index, span, :]
                + jnp.dot(ref[...], held[index], preferred_element_type=F32)
                for index in (2 * core, 2 * core + 1)
            ]
            hidden_ref[core, span, :] = (gate * jax.nn.sigmoid(gate) * up).astype(BF16)
    copies[4].wait()
    copies[5].wait()
    for part in range(2):
        span = slice(part * rows, (part + 1) * rows)
        out_ref[part] = (
            jnp.dot(hidden_ref[0, span, :], held_down[0], preferred_element_type=F32)
            + jnp.dot(hidden_ref[1, span, :], held_down[1], preferred_element_type=F32)
        ).astype(BF16)


def down(hidden_ref, span, w0, w1, where):
    return jnp.dot(hidden_ref[0, span, :], w0[:, where], preferred_element_type=F32) + jnp.dot(
        hidden_ref[1, span, :], w1[:, where], preferred_element_type=F32
    )


def direct_kernel(quarter_ref, hidden_ref, w0, w1, right_ref, left_ref):
    rows, width = right_ref.shape
    blocks = w0.shape[1] // width
    right = down(hidden_ref, slice(rows, None), w0, w1, cut(quarter_ref, 1, blocks, width))
    left = down(hidden_ref, slice(0, rows), w0, w1, cut(quarter_ref, blocks - 1, blocks, width))
    right_ref[...] = right.astype(BF16)
    left_ref[...] = left.astype(BF16)


def relay_kernel(quarter_ref, hidden_ref, w0, w1, top_ref, bottom_ref, right_ref, left_ref):
    rows, width = right_ref.shape
    blocks = w0.shape[1] // width
    right = down(hidden_ref, slice(0, rows), w0, w1, cut(quarter_ref, 1, blocks, width))
    left = down(hidden_ref, slice(rows, None), w0, w1, cut(quarter_ref, blocks - 1, blocks, width))
    right_ref[...] = (right + top_ref[...].astype(F32)).astype(BF16)
    left_ref[...] = (left + bottom_ref[...].astype(F32)).astype(BF16)


def own_kernel(quarter_ref, hidden_ref, w0, w1, out_ref):
    width = out_ref.shape[1]
    where = cut(quarter_ref, 0, w0.shape[1] // width, width)
    out_ref[...] = down(hidden_ref, slice(None), w0, w1, where)


def sum_kernel(own_ref, l0, l1, r0, r1, out_ref):
    rows = l0.shape[0]
    for part, (l_ref, r_ref) in enumerate(((l0, r0), (l1, r1))):
        span = slice(part * rows, (part + 1) * rows)
        total = own_ref[span, :] + l_ref[...].astype(F32) + r_ref[...].astype(F32)
        out_ref[span, :] = total.astype(BF16)


def combine_kernel(slots_ref, route_ref, out_ref):
    count = slots_ref.shape[0]
    everything = route_ref.shape[1]
    slot = lax.broadcasted_iota(jnp.int32, (count, everything), 0)
    first = slot == route_ref[0:1].astype(jnp.int32)
    second = slot == route_ref[1:2].astype(jnp.int32)
    high = jnp.where(first, route_ref[2:3], 0.0) + jnp.where(second, route_ref[4:5], 0.0)
    low = jnp.where(first, route_ref[3:4], 0.0) + jnp.where(second, route_ref[5:6], 0.0)
    rows = slots_ref[...]
    dims = (((0,), (0,)), ((), ()))
    mixed = lax.dot_general(high.astype(BF16), rows, dims, preferred_element_type=F32)
    mixed = mixed + lax.dot_general(low.astype(BF16), rows, dims, preferred_element_type=F32)
    mixed = mixed.astype(BF16)
    tokens = out_ref.shape[1]
    for member in range(out_ref.shape[0]):
        out_ref[member] = mixed[member * PAD : member * PAD + tokens, :]


def gate_kernel(parts_ref, modulation_ref, out_ref):
    lanes = parts_ref.shape[2]
    for quarter in range(parts_ref.shape[0] // CORES):
        total = parts_ref[CORES * quarter].astype(F32)
        for core in range(1, CORES):
            total = total + parts_ref[CORES * quarter + core].astype(F32)
        cols = slice(quarter * lanes, (quarter + 1) * lanes)
        out_ref[:, cols] = (modulation_ref[2][:, cols] * total).astype(BF16)


def body(tokens, modulation, w_router, gate_weight, up_weight, down_weight, expert_ids):
    chips = lax.axis_size("x")
    members = chips * CORES
    own, width = tokens.shape
    lanes = width // chips
    experts = w_router.shape[1]
    images = lax.axis_size("expert")
    half = SLOT // CORES
    count = experts * half
    x = lax.axis_index("x")
    core = lax.axis_index("c")
    tensor = ("x", "c")
    swap = [(0, 1), (1, 0)]
    weights = [gate_weight[0], up_weight[0], down_weight[0]]
    others = [lax.ppermute(w, "c", swap) for w in weights]

    shift_scale_gate = jnp.transpose(modulation, (1, 0, 2))
    packet = call(
        modulate_kernel,
        jax.ShapeDtypeStruct((members, PAD, lanes), BF16),
        2 * own * width * experts,
        4 * own * width,
        "vvhhh",
        [
            pltpu.VMEM(tokens.shape, BF16),
            pltpu.VMEM(shift_scale_gate.shape, F32),
            pltpu.VMEM((experts, width), BF16),
            pltpu.SemaphoreType.DMA((3,)),
        ],
        FIRST_LIMIT,
    )(
        (x * CORES + core).astype(jnp.int32).reshape(1),
        expert_ids.T,
        tokens,
        shift_scale_gate,
        w_router.T,
    )
    packet = lax.all_to_all(packet, tensor, 0, 0, tiled=True)
    slots, route = call(
        fill_kernel,
        (
            jax.ShapeDtypeStruct((count, lanes), BF16),
            jax.ShapeDtypeStruct((8, members * PAD), F32),
        ),
        2 * count * members * PAD * lanes,
        4 * count * lanes,
    )(core.astype(jnp.int32).reshape(1), packet)
    arrived = lax.all_to_all(
        slots.reshape(experts, half, lanes), "expert", 0, 0, tiled=True
    ).reshape(count, lanes)

    quarter = x.astype(jnp.int32).reshape(1)
    onward = [(i, (i + 1) % chips) for i in range(chips)]
    backward = [(i, (i - 1) % chips) for i in range(chips)]
    g0, u0, w0 = weights
    g1, u1, w1 = others
    cols = gate_weight.shape[2]
    cut_rows = count // 2
    upper, lower = arrived[:cut_rows], arrived[cut_rows:]
    l0 = lax.ppermute(upper, "x", onward)
    r1 = lax.ppermute(lower, "x", backward)
    l1 = lax.ppermute(lower, "x", onward)
    r0 = lax.ppermute(upper, "x", backward)
    top = lax.ppermute(l0, "x", onward)
    bottom = lax.ppermute(r1, "x", backward)
    near = call(
        near_kernel,
        jax.ShapeDtypeStruct((4, count, cols), F32),
        24 * count * lanes * cols,
        16 * lanes * cols + 16 * count * cols,
        "vvvvvvhhhh",
        [pltpu.VMEM((4, 3, lanes, cols), BF16), pltpu.SemaphoreType.DMA((4, 3))],
    )(quarter, arrived, l0, l1, r0, r1, g0, u0, g1, u1)
    hidden, far = call(
        far_kernel,
        (
            jax.ShapeDtypeStruct((2, count, cols), BF16),
            jax.ShapeDtypeStruct((2, cut_rows, lanes), BF16),
        ),
        12 * count * lanes * cols,
        16 * count * cols,
        "vvvvhhhhhh",
        [
            pltpu.VMEM((4, lanes, cols), BF16),
            pltpu.VMEM((2, cols, lanes), BF16),
            pltpu.SemaphoreType.DMA((6,)),
        ],
    )(quarter, near, top, bottom, g0, u0, g1, u1, w0, w1)
    top = lax.ppermute(far[0], "x", onward)
    bottom = lax.ppermute(far[1], "x", backward)
    piece = jax.ShapeDtypeStruct((cut_rows, lanes), BF16)
    direct_right, direct_left = call(
        direct_kernel, (piece, piece), 4 * count * lanes * cols, 4 * count * lanes
    )(quarter, hidden, w0, w1)
    l1 = lax.ppermute(direct_right, "x", onward)
    r0 = lax.ppermute(direct_left, "x", backward)
    to_right, to_left = call(
        relay_kernel, (piece, piece), 4 * count * lanes * cols, 4 * count * lanes
    )(quarter, hidden, w0, w1, top, bottom)
    l0 = lax.ppermute(to_right, "x", onward)
    r1 = lax.ppermute(to_left, "x", backward)
    own_sum = call(
        own_kernel,
        jax.ShapeDtypeStruct((count, lanes), F32),
        4 * count * lanes * cols,
        4 * count * lanes,
    )(quarter, hidden, w0, w1)
    summed = call(
        sum_kernel,
        jax.ShapeDtypeStruct((count, lanes), BF16),
        2 * count * lanes,
        10 * count * lanes,
    )(own_sum, l0, l1, r0, r1)
    produced = lax.all_to_all(
        summed.reshape(images, half, lanes), "expert", 0, 0, tiled=True
    ).reshape(count, lanes)
    mixed = call(
        combine_kernel,
        jax.ShapeDtypeStruct((members, own, lanes), BF16),
        4 * count * members * PAD * lanes,
        4 * count * lanes,
    )(produced, route)
    mixed = lax.all_to_all(mixed, tensor, 0, 0, tiled=True)
    return call(
        gate_kernel, jax.ShapeDtypeStruct((own, width), BF16), own * width, 4 * own * width
    )(mixed, shift_scale_gate)


def solution(mesh):
    images, members = mesh.devices.shape
    fine = Mesh(mesh.devices.reshape(images, members // CORES, CORES), ("expert", "x", "c"))
    tensor = ("x", "c")
    rows = P(("expert", "x", "c"), None)
    placed = (
        rows,
        P("expert", None, None),
        P(),
        P("expert", None, tensor),
        P("expert", None, tensor),
        P("expert", tensor, None),
        rows,
    )
    return jax.shard_map(body, mesh=fine, in_specs=placed, out_specs=rows, check_vma=False)
```

```python
import functools

import jax
import jax.numpy as jnp
from jax import lax
from jax.experimental import pallas as pl
from jax.experimental.pallas import tpu as pltpu
from jax.sharding import Mesh, PartitionSpec as P

EPS = 1e-06
F32 = jnp.float32
BF16 = jnp.bfloat16
CORES = 2
SLOT = 16
PAD = 64
ROUTE = 16
VMEM_LIMIT = 12 * 1024 * 1024
FIRST_LIMIT = 60 * 1024 * 1024


def call(kernel, out_shape, flops, nbytes, spaces=None, scratch=(), limit=VMEM_LIMIT):
    kinds = {"v": pltpu.VMEM, "h": pltpu.HBM}
    specs = {}
    if spaces is not None:
        specs = {"in_specs": [pl.BlockSpec(memory_space=kinds[kind]) for kind in spaces]}
    return pl.pallas_call(
        kernel,
        out_shape=out_shape,
        scratch_shapes=scratch,
        compiler_params=pltpu.CompilerParams(vmem_limit_bytes=limit),
        cost_estimate=pl.CostEstimate(flops=flops, bytes_accessed=nbytes, transcendentals=0),
        **specs,
    )


def high_low(value):
    high = value.astype(BF16).astype(F32)
    return high, value - high


def modulate_kernel(
    member_ref, ids_ref, tokens_in, modulation_in, router_in, packet_ref,
    tokens_ref, modulation_ref, router_ref, arrived,
):
    copies = [
        pltpu.make_async_copy(source, target, arrived.at[index])
        for index, (source, target) in enumerate(
            ((tokens_in, tokens_ref), (modulation_in, modulation_ref), (router_in, router_ref))
        )
    ]
    for copy in copies:
        copy.start()
    copies[0].wait()
    rows, width = tokens_ref.shape
    lanes = packet_ref.shape[2]
    values = tokens_ref[...].astype(F32)
    average = jnp.mean(values, axis=-1, keepdims=True)
    centred = values - average
    spread = jnp.mean(centred * centred, axis=-1, keepdims=True)
    normed = centred * lax.rsqrt(spread + EPS)
    copies[1].wait()
    copies[2].wait()
    modulated = (normed * (1.0 + modulation_ref[1]) + modulation_ref[0]).astype(BF16)
    logits = lax.dot_general(
        router_ref[...], modulated, (((1,), (1,)), ((), ())), preferred_element_type=F32
    )
    chance_all = jax.nn.sigmoid(logits)
    expert = lax.broadcasted_iota(jnp.int32, logits.shape, 0)
    ids = ids_ref[...]
    chance = [
        jnp.sum(jnp.where(expert == ids[c : c + 1], chance_all, 0.0), axis=0, keepdims=True)
        for c in range(2)
    ]
    total = chance[0] + chance[1]
    first_high, first_low = high_low(chance[0] / total)
    second_high, second_low = high_low(chance[1] / total)
    named = ids.astype(F32)
    route = jnp.concatenate(
        [
            named[0:1] + 1.0,
            named[1:2] + 1.0,
            first_high,
            first_low,
            second_high,
            second_low,
            jnp.zeros((ROUTE - 6, rows), F32),
        ],
        axis=0,
    ).astype(BF16)
    token = lax.broadcasted_iota(jnp.int32, (rows, lanes), 0)
    lane = lax.broadcasted_iota(jnp.int32, (rows, lanes), 1)
    place = jnp.where(lane == token + member_ref[0] * PAD, 1.0, 0.0).astype(BF16)
    placed = jnp.dot(route, place, preferred_element_type=F32).astype(BF16)
    for member in range(packet_ref.shape[0]):
        quarter = member // CORES
        packet_ref[member, 0:rows, :] = modulated[:, quarter * lanes : (quarter + 1) * lanes]
        packet_ref[member, rows:PAD, :] = placed


def fill_kernel(core_ref, packet_ref, slots_ref, route_ref):
    members, _, lanes = packet_ref.shape
    count = slots_ref.shape[0]
    half = SLOT // CORES
    experts = count // half
    tokens = PAD - ROUTE
    route = packet_ref[0, tokens:PAD, :].astype(F32)
    for member in range(1, members):
        route = route + packet_ref[member, tokens:PAD, :].astype(F32)
    everything = packet_ref.shape[0] * PAD
    named = [route[c : c + 1].astype(jnp.int32) - 1 for c in range(2)]
    expert = lax.broadcasted_iota(jnp.int32, (experts, everything), 0)
    names = [expert == named[c] for c in range(2)]
    either = jnp.where(names[0] | names[1], 1.0, 0.0).astype(BF16)
    earlier = lax.broadcasted_iota(jnp.int32, (everything, everything), 0) < (
        lax.broadcasted_iota(jnp.int32, (everything, everything), 1)
    )
    before = jnp.dot(
        either, jnp.where(earlier, 1.0, 0.0).astype(BF16), preferred_element_type=F32
    )
    place = []
    for c in range(2):
        position = jnp.sum(jnp.where(names[c], before, 0.0), axis=0, keepdims=True)
        position = position.astype(jnp.int32) - core_ref[0] * half
        here = (position >= 0) & (position < half) & (named[c] >= 0)
        place.append(jnp.where(here, named[c] * half + position, -1))
    slot = lax.broadcasted_iota(jnp.int32, (count, everything), 0)
    pick = jnp.where((slot == place[0]) | (slot == place[1]), 1.0, 0.0).astype(BF16)
    rows = packet_ref[...].reshape(everything, lanes)
    slots_ref[...] = jnp.dot(pick, rows, preferred_element_type=F32).astype(BF16)
    route_ref[...] = jnp.concatenate(
        [place[0].astype(F32), place[1].astype(F32), route[2:6], jnp.zeros((2, everything), F32)],
        axis=0,
    )


def cut(place_ref, index, width):
    return pl.ds(pl.multiple_of(place_ref[index] * width, width), width)


def copy_kernel(source_ref, after_ref, out_ref):
    out_ref[...] = source_ref[...]


def near_kernel(place_ref, a_ref, m_ref, g0, u0, g1, u1, out_ref, held, arrived):
    width = a_ref.shape[1]
    copies = [
        [
            pltpu.make_async_copy(
                weight_ref.at[cut(place_ref, place, width), :],
                held.at[index, place],
                arrived.at[index, place],
            )
            for place in range(2)
        ]
        for index, weight_ref in enumerate((g0, u0, g1, u1))
    ]
    for group in copies:
        for copy in group:
            copy.start()
    for index, group in enumerate(copies):
        for copy in group:
            copy.wait()
        out_ref[index] = jnp.dot(
            a_ref[...], held[index, 0], preferred_element_type=F32
        ) + jnp.dot(m_ref[...], held[index, 1], preferred_element_type=F32)


def far_kernel(
    place_ref, near_ref, n_ref, f_ref, g0, u0, g1, u1, w0, w1,
    hidden_ref, out_ref, held, held_down, arrived,
):
    width = f_ref.shape[1]
    where = cut(place_ref, 3, width)
    copies = [
        pltpu.make_async_copy(
            weight_ref.at[cut(place_ref, 2 + part, width), :],
            held.at[index, part],
            arrived.at[2 * index + part],
        )
        for index, weight_ref in enumerate((g0, u0, g1, u1))
        for part in range(2)
    ] + [
        pltpu.make_async_copy(down_ref.at[:, where], held_down.at[core], arrived.at[8 + core])
        for core, down_ref in enumerate((w0, w1))
    ]
    for copy in copies:
        copy.start()
    for core in range(2):
        for copy in copies[4 * core : 4 * core + 4]:
            copy.wait()
        gate, up = [
            near_ref[index]
            + jnp.dot(n_ref[...], held[index, 0], preferred_element_type=F32)
            + jnp.dot(f_ref[...], held[index, 1], preferred_element_type=F32)
            for index in (2 * core, 2 * core + 1)
        ]
        hidden_ref[core] = (gate * jax.nn.sigmoid(gate) * up).astype(BF16)
    copies[8].wait()
    copies[9].wait()
    out_ref[...] = (
        jnp.dot(hidden_ref[0], held_down[0], preferred_element_type=F32)
        + jnp.dot(hidden_ref[1], held_down[1], preferred_element_type=F32)
    ).astype(BF16)


def down(hidden_ref, w0, w1, where):
    return jnp.dot(hidden_ref[0], w0[:, where], preferred_element_type=F32) + jnp.dot(
        hidden_ref[1], w1[:, where], preferred_element_type=F32
    )


def direct_kernel(place_ref, hidden_ref, w0, w1, out_ref):
    where = cut(place_ref, 1, out_ref.shape[1])
    out_ref[...] = down(hidden_ref, w0, w1, where).astype(BF16)


def relay_kernel(place_ref, hidden_ref, w0, w1, came_ref, direct_ref, out_ref, again_ref):
    where = cut(place_ref, 2, out_ref.shape[1])
    again_ref[...] = direct_ref[...]
    out_ref[...] = (down(hidden_ref, w0, w1, where) + came_ref[...].astype(F32)).astype(BF16)


def own_kernel(place_ref, hidden_ref, w0, w1, out_ref):
    out_ref[...] = down(hidden_ref, w0, w1, cut(place_ref, 0, out_ref.shape[1]))


def sum_kernel(own_ref, major_ref, minor_ref, out_ref):
    total = own_ref[...] + major_ref[...].astype(F32) + minor_ref[...].astype(F32)
    out_ref[...] = total.astype(BF16)


def combine_kernel(slots_ref, route_ref, out_ref):
    count = slots_ref.shape[0]
    everything = route_ref.shape[1]
    slot = lax.broadcasted_iota(jnp.int32, (count, everything), 0)
    first = slot == route_ref[0:1].astype(jnp.int32)
    second = slot == route_ref[1:2].astype(jnp.int32)
    high = jnp.where(first, route_ref[2:3], 0.0) + jnp.where(second, route_ref[4:5], 0.0)
    low = jnp.where(first, route_ref[3:4], 0.0) + jnp.where(second, route_ref[5:6], 0.0)
    rows = slots_ref[...]
    dims = (((0,), (0,)), ((), ()))
    mixed = lax.dot_general(high.astype(BF16), rows, dims, preferred_element_type=F32)
    mixed = mixed + lax.dot_general(low.astype(BF16), rows, dims, preferred_element_type=F32)
    mixed = mixed.astype(BF16)
    tokens = out_ref.shape[1]
    for member in range(out_ref.shape[0]):
        out_ref[member] = mixed[member * PAD : member * PAD + tokens, :]


def gate_kernel(parts_ref, modulation_ref, out_ref):
    lanes = parts_ref.shape[2]
    for quarter in range(parts_ref.shape[0] // CORES):
        total = parts_ref[CORES * quarter].astype(F32)
        for core in range(1, CORES):
            total = total + parts_ref[CORES * quarter + core].astype(F32)
        cols = slice(quarter * lanes, (quarter + 1) * lanes)
        out_ref[:, cols] = (modulation_ref[2][:, cols] * total).astype(BF16)


def body(tokens, modulation, w_router, gate_weight, up_weight, down_weight, expert_ids):
    chips = lax.axis_size("x")
    members = chips * CORES
    own, width = tokens.shape
    lanes = width // chips
    experts = w_router.shape[1]
    images = lax.axis_size("expert")
    half = SLOT // CORES
    count = experts * half
    x = lax.axis_index("x")
    core = lax.axis_index("c")
    tensor = ("x", "c")
    swap = [(0, 1), (1, 0)]
    weights = [gate_weight[0], up_weight[0], down_weight[0]]
    others = [lax.ppermute(w, "c", swap) for w in weights]

    shift_scale_gate = jnp.transpose(modulation, (1, 0, 2))
    packet = call(
        modulate_kernel,
        jax.ShapeDtypeStruct((members, PAD, lanes), BF16),
        2 * own * width * experts,
        4 * own * width,
        "vvhhh",
        [
            pltpu.VMEM(tokens.shape, BF16),
            pltpu.VMEM(shift_scale_gate.shape, F32),
            pltpu.VMEM((experts, width), BF16),
            pltpu.SemaphoreType.DMA((3,)),
        ],
        FIRST_LIMIT,
    )(
        (x * CORES + core).astype(jnp.int32).reshape(1),
        expert_ids.T,
        tokens,
        shift_scale_gate,
        w_router.T,
    )
    packet = lax.all_to_all(packet, tensor, 0, 0, tiled=True)
    slots, route = call(
        fill_kernel,
        (
            jax.ShapeDtypeStruct((count, lanes), BF16),
            jax.ShapeDtypeStruct((8, members * PAD), F32),
        ),
        2 * count * members * PAD * lanes,
        4 * count * lanes,
    )(core.astype(jnp.int32).reshape(1), packet)
    arrived = lax.all_to_all(
        slots.reshape(experts, half, lanes), "expert", 0, 0, tiled=True
    ).reshape(count, lanes)

    major = [
        (i * CORES + c, (i + 1 - 2 * c) % chips * CORES + c)
        for i in range(chips)
        for c in range(CORES)
    ]
    minor = [(target, source) for source, target in major]
    step = (1 - 2 * core).astype(jnp.int32)
    at = x.astype(jnp.int32) + chips
    place = jnp.stack([at, at - step, at + step, at + 2]) % chips
    g0, u0, w0 = weights
    g1, u1, w1 = others
    cols = gate_weight.shape[2]
    from_major = lax.ppermute(arrived, tensor, major)
    from_far = lax.ppermute(from_major, tensor, major)
    again = call(copy_kernel, jax.ShapeDtypeStruct(arrived.shape, BF16), 0, 4 * count * lanes, "vh")(arrived, from_major)
    from_minor = lax.ppermute(again, tensor, minor)
    near = call(
        near_kernel,
        jax.ShapeDtypeStruct((4, count, cols), F32),
        24 * count * lanes * cols,
        16 * lanes * cols + 16 * count * cols,
        "vvvhhhh",
        [pltpu.VMEM((4, 2, lanes, cols), BF16), pltpu.SemaphoreType.DMA((4, 2))],
    )(place, arrived, from_major, g0, u0, g1, u1)
    piece = jax.ShapeDtypeStruct((count, lanes), BF16)
    hidden, far = call(
        far_kernel,
        (jax.ShapeDtypeStruct((2, count, cols), BF16), piece),
        12 * count * lanes * cols,
        16 * count * cols,
        "vvvvhhhhhh",
        [
            pltpu.VMEM((4, 2, lanes, cols), BF16),
            pltpu.VMEM((2, cols, lanes), BF16),
            pltpu.SemaphoreType.DMA((10,)),
        ],
    )(place, near, from_minor, from_far, g0, u0, g1, u1, w0, w1)
    work = (4 * count * lanes * cols, 4 * count * lanes)
    came = lax.ppermute(far, tensor, major)
    direct = call(direct_kernel, piece, *work)(place, hidden, w0, w1)
    relayed, direct = call(relay_kernel, (piece, piece), *work)(
        place, hidden, w0, w1, came, direct
    )
    from_major = lax.ppermute(relayed, tensor, major)
    from_minor = lax.ppermute(direct, tensor, minor)
    own_sum = call(own_kernel, jax.ShapeDtypeStruct((count, lanes), F32), *work)(
        place, hidden, w0, w1
    )
    summed = call(sum_kernel, piece, 2 * count * lanes, 8 * count * lanes)(
        own_sum, from_major, from_minor
    )
    produced = lax.all_to_all(
        summed.reshape(images, half, lanes), "expert", 0, 0, tiled=True
    ).reshape(count, lanes)
    mixed = call(
        combine_kernel,
        jax.ShapeDtypeStruct((members, own, lanes), BF16),
        4 * count * members * PAD * lanes,
        4 * count * lanes,
    )(produced, route)
    mixed = lax.all_to_all(mixed, tensor, 0, 0, tiled=True)
    return call(
        gate_kernel, jax.ShapeDtypeStruct((own, width), BF16), own * width, 4 * own * width
    )(mixed, shift_scale_gate)


def solution(mesh):
    images, members = mesh.devices.shape
    fine = Mesh(mesh.devices.reshape(images, members // CORES, CORES), ("expert", "x", "c"))
    tensor = ("x", "c")
    rows = P(("expert", "x", "c"), None)
    placed = (
        rows,
        P("expert", None, None),
        P(),
        P("expert", None, tensor),
        P("expert", None, tensor),
        P("expert", tensor, None),
        rows,
    )
    return jax.shard_map(body, mesh=fine, in_specs=placed, out_specs=rows, check_vma=False)
```

```python
import functools

import jax
import jax.numpy as jnp
from jax import lax
from jax.experimental import pallas as pl
from jax.experimental.pallas import tpu as pltpu
from jax.sharding import Mesh, PartitionSpec as P

EPS = 1e-06
F32 = jnp.float32
BF16 = jnp.bfloat16
CORES = 2
SLOT = 16
PAD = 64
ROUTE = 16
VMEM_LIMIT = 12 * 1024 * 1024
FIRST_LIMIT = 60 * 1024 * 1024


def call(kernel, out_shape, flops, nbytes, spaces=None, scratch=(), limit=VMEM_LIMIT):
    kinds = {"v": pltpu.VMEM, "h": pltpu.HBM, "s": pltpu.SMEM}
    specs = {}
    if spaces is not None:
        specs = {"in_specs": [pl.BlockSpec(memory_space=kinds[kind]) for kind in spaces]}
    return pl.pallas_call(
        kernel,
        out_shape=out_shape,
        scratch_shapes=scratch,
        compiler_params=pltpu.CompilerParams(vmem_limit_bytes=limit),
        cost_estimate=pl.CostEstimate(flops=flops, bytes_accessed=nbytes, transcendentals=0),
        **specs,
    )


def high_low(value):
    high = value.astype(BF16).astype(F32)
    return high, value - high


def modulate_kernel(
    member_ref, ids_in, tokens_in, modulation_in, router_in, packet_ref,
    tokens_ref, modulation_ref, router_ref, ids_ref, arrived,
):
    copies = [
        pltpu.make_async_copy(source, target, arrived.at[index])
        for index, (source, target) in enumerate(
            (
                (tokens_in, tokens_ref),
                (modulation_in, modulation_ref),
                (router_in, router_ref),
                (ids_in, ids_ref),
            )
        )
    ]
    for copy in copies:
        copy.start()
    copies[0].wait()
    rows, width = tokens_ref.shape
    lanes = packet_ref.shape[2]
    values = tokens_ref[...].astype(F32)
    average = jnp.mean(values, axis=-1, keepdims=True)
    centred = values - average
    spread = jnp.mean(centred * centred, axis=-1, keepdims=True)
    normed = centred * lax.rsqrt(spread + EPS)
    copies[1].wait()
    copies[2].wait()
    copies[3].wait()
    modulated = (normed * (1.0 + modulation_ref[1]) + modulation_ref[0]).astype(BF16)
    logits = lax.dot_general(
        router_ref[...], modulated, (((1,), (1,)), ((), ())), preferred_element_type=F32
    )
    chance_all = jax.nn.sigmoid(logits)
    expert = lax.broadcasted_iota(jnp.int32, logits.shape, 0)
    ids = ids_ref[...]
    chance = [
        jnp.sum(jnp.where(expert == ids[c : c + 1], chance_all, 0.0), axis=0, keepdims=True)
        for c in range(2)
    ]
    total = chance[0] + chance[1]
    first_high, first_low = high_low(chance[0] / total)
    second_high, second_low = high_low(chance[1] / total)
    named = ids.astype(F32)
    route = jnp.concatenate(
        [
            named[0:1] + 1.0,
            named[1:2] + 1.0,
            first_high,
            first_low,
            second_high,
            second_low,
            jnp.zeros((ROUTE - 6, rows), F32),
        ],
        axis=0,
    ).astype(BF16)
    token = lax.broadcasted_iota(jnp.int32, (rows, lanes), 0)
    lane = lax.broadcasted_iota(jnp.int32, (rows, lanes), 1)
    place = jnp.where(lane == token + member_ref[0] * PAD, 1.0, 0.0).astype(BF16)
    placed = jnp.dot(route, place, preferred_element_type=F32).astype(BF16)
    for member in range(packet_ref.shape[0]):
        quarter = member // CORES
        packet_ref[member, 0:rows, :] = modulated[:, quarter * lanes : (quarter + 1) * lanes]
        packet_ref[member, rows:PAD, :] = placed


def fill_kernel(core_ref, packet_ref, slots_ref, route_ref):
    members, _, lanes = packet_ref.shape
    count = slots_ref.shape[0]
    half = SLOT // CORES
    experts = count // half
    tokens = PAD - ROUTE
    route = packet_ref[0, tokens:PAD, :].astype(F32)
    for member in range(1, members):
        route = route + packet_ref[member, tokens:PAD, :].astype(F32)
    everything = packet_ref.shape[0] * PAD
    named = [route[c : c + 1].astype(jnp.int32) - 1 for c in range(2)]
    expert = lax.broadcasted_iota(jnp.int32, (experts, everything), 0)
    names = [expert == named[c] for c in range(2)]
    either = jnp.where(names[0] | names[1], 1.0, 0.0).astype(BF16)
    earlier = lax.broadcasted_iota(jnp.int32, (everything, everything), 0) < (
        lax.broadcasted_iota(jnp.int32, (everything, everything), 1)
    )
    before = jnp.dot(
        either, jnp.where(earlier, 1.0, 0.0).astype(BF16), preferred_element_type=F32
    )
    place = []
    for c in range(2):
        position = jnp.sum(jnp.where(names[c], before, 0.0), axis=0, keepdims=True)
        position = position.astype(jnp.int32) - core_ref[0] * half
        here = (position >= 0) & (position < half) & (named[c] >= 0)
        place.append(jnp.where(here, named[c] * half + position, -1))
    slot = lax.broadcasted_iota(jnp.int32, (count, everything), 0)
    pick = jnp.where((slot == place[0]) | (slot == place[1]), 1.0, 0.0).astype(BF16)
    rows = packet_ref[...].reshape(everything, lanes)
    slots_ref[...] = jnp.dot(pick, rows, preferred_element_type=F32).astype(BF16)
    route_ref[...] = jnp.concatenate(
        [place[0].astype(F32), place[1].astype(F32), route[2:6], jnp.zeros((2, everything), F32)],
        axis=0,
    )


def cut(quarter_ref, step, blocks, width):
    return pl.ds(pl.multiple_of(lax.rem(quarter_ref[0] + step, blocks) * width, width), width)


def near_kernel(quarter_ref, a_ref, l0, l1, r0, r1, g0, u0, g1, u1, out_ref, held, arrived):
    rows, width = l0.shape
    blocks = g0.shape[0] // width
    copies = [
        [
            pltpu.make_async_copy(
                weight_ref.at[cut(quarter_ref, step, blocks, width), :],
                held.at[index, place],
                arrived.at[index, place],
            )
            for place, step in enumerate((0, blocks - 1, 1))
        ]
        for index, weight_ref in enumerate((g0, u0, g1, u1))
    ]
    for group in copies:
        for copy in group:
            copy.start()
    for index, group in enumerate(copies):
        for copy in group:
            copy.wait()
        for part, (l_ref, r_ref) in enumerate(((l0, r0), (l1, r1))):
            span = slice(part * rows, (part + 1) * rows)
            out_ref[index, span, :] = (
                jnp.dot(a_ref[span, :], held[index, 0], preferred_element_type=F32)
                + jnp.dot(l_ref[...], held[index, 1], preferred_element_type=F32)
                + jnp.dot(r_ref[...], held[index, 2], preferred_element_type=F32)
            )


def far_kernel(
    quarter_ref, near_ref, top_ref, bottom_ref, g0, u0, g1, u1, w0, w1,
    hidden_ref, out_ref, held, held_down, arrived,
):
    rows, width = top_ref.shape
    blocks = g0.shape[0] // width
    where = cut(quarter_ref, blocks // 2, blocks, width)
    copies = [
        pltpu.make_async_copy(weight_ref.at[where, :], held.at[index], arrived.at[index])
        for index, weight_ref in enumerate((g0, u0, g1, u1))
    ] + [
        pltpu.make_async_copy(down_ref.at[:, where], held_down.at[core], arrived.at[4 + core])
        for core, down_ref in enumerate((w0, w1))
    ]
    for copy in copies:
        copy.start()
    for core in range(2):
        copies[2 * core].wait()
        copies[2 * core + 1].wait()
        for part, ref in enumerate((top_ref, bottom_ref)):
            span = slice(part * rows, (part + 1) * rows)
            gate, up = [
                near_ref[index, span, :]
                + jnp.dot(ref[...], held[index], preferred_element_type=F32)
                for index in (2 * core, 2 * core + 1)
            ]
            hidden_ref[core, span, :] = (gate * jax.nn.sigmoid(gate) * up).astype(BF16)
    copies[4].wait()
    copies[5].wait()
    for part in range(2):
        span = slice(part * rows, (part + 1) * rows)
        out_ref[part] = (
            jnp.dot(hidden_ref[0, span, :], held_down[0], preferred_element_type=F32)
            + jnp.dot(hidden_ref[1, span, :], held_down[1], preferred_element_type=F32)
        ).astype(BF16)


def down(hidden_ref, span, w0, w1, where):
    return jnp.dot(hidden_ref[0, span, :], w0[:, where], preferred_element_type=F32) + jnp.dot(
        hidden_ref[1, span, :], w1[:, where], preferred_element_type=F32
    )


def direct_kernel(quarter_ref, hidden_ref, w0, w1, right_ref, left_ref):
    rows, width = right_ref.shape
    blocks = w0.shape[1] // width
    right = down(hidden_ref, slice(rows, None), w0, w1, cut(quarter_ref, 1, blocks, width))
    left = down(hidden_ref, slice(0, rows), w0, w1, cut(quarter_ref, blocks - 1, blocks, width))
    right_ref[...] = right.astype(BF16)
    left_ref[...] = left.astype(BF16)


def relay_kernel(quarter_ref, hidden_ref, w0, w1, top_ref, bottom_ref, right_ref, left_ref):
    rows, width = right_ref.shape
    blocks = w0.shape[1] // width
    right = down(hidden_ref, slice(0, rows), w0, w1, cut(quarter_ref, 1, blocks, width))
    left = down(hidden_ref, slice(rows, None), w0, w1, cut(quarter_ref, blocks - 1, blocks, width))
    right_ref[...] = (right + top_ref[...].astype(F32)).astype(BF16)
    left_ref[...] = (left + bottom_ref[...].astype(F32)).astype(BF16)


def own_kernel(quarter_ref, hidden_ref, w0, w1, out_ref):
    width = out_ref.shape[1]
    where = cut(quarter_ref, 0, w0.shape[1] // width, width)
    out_ref[...] = down(hidden_ref, slice(None), w0, w1, where)


def sum_kernel(own_ref, l0, l1, r0, r1, out_ref):
    rows = l0.shape[0]
    for part, (l_ref, r_ref) in enumerate(((l0, r0), (l1, r1))):
        span = slice(part * rows, (part + 1) * rows)
        total = own_ref[span, :] + l_ref[...].astype(F32) + r_ref[...].astype(F32)
        out_ref[span, :] = total.astype(BF16)


def combine_kernel(slots_ref, route_ref, out_ref):
    count = slots_ref.shape[0]
    everything = route_ref.shape[1]
    slot = lax.broadcasted_iota(jnp.int32, (count, everything), 0)
    first = slot == route_ref[0:1].astype(jnp.int32)
    second = slot == route_ref[1:2].astype(jnp.int32)
    high = jnp.where(first, route_ref[2:3], 0.0) + jnp.where(second, route_ref[4:5], 0.0)
    low = jnp.where(first, route_ref[3:4], 0.0) + jnp.where(second, route_ref[5:6], 0.0)
    rows = slots_ref[...]
    dims = (((0,), (0,)), ((), ()))
    mixed = lax.dot_general(high.astype(BF16), rows, dims, preferred_element_type=F32)
    mixed = mixed + lax.dot_general(low.astype(BF16), rows, dims, preferred_element_type=F32)
    mixed = mixed.astype(BF16)
    tokens = out_ref.shape[1]
    for member in range(out_ref.shape[0]):
        out_ref[member] = mixed[member * PAD : member * PAD + tokens, :]


def gate_kernel(parts_ref, modulation_ref, out_ref):
    lanes = parts_ref.shape[2]
    for quarter in range(parts_ref.shape[0] // CORES):
        total = parts_ref[CORES * quarter].astype(F32)
        for core in range(1, CORES):
            total = total + parts_ref[CORES * quarter + core].astype(F32)
        cols = slice(quarter * lanes, (quarter + 1) * lanes)
        out_ref[:, cols] = (modulation_ref[2][:, cols] * total).astype(BF16)


def body(tokens, modulation, w_router, gate_weight, up_weight, down_weight, expert_ids):
    chips = lax.axis_size("x")
    members = chips * CORES
    own, width = tokens.shape
    lanes = width // chips
    experts = w_router.shape[1]
    images = lax.axis_size("expert")
    half = SLOT // CORES
    count = experts * half
    x = lax.axis_index("x")
    core = lax.axis_index("c")
    tensor = ("x", "c")
    swap = [(0, 1), (1, 0)]
    weights = [gate_weight[0], up_weight[0], down_weight[0]]
    others = [lax.ppermute(w, "c", swap) for w in weights]

    shift_scale_gate = jnp.transpose(modulation, (1, 0, 2))
    packet = call(
        modulate_kernel,
        jax.ShapeDtypeStruct((members, PAD, lanes), BF16),
        2 * own * width * experts,
        4 * own * width,
        "shhhh",
        [
            pltpu.VMEM(tokens.shape, BF16),
            pltpu.VMEM(shift_scale_gate.shape, F32),
            pltpu.VMEM((experts, width), BF16),
            pltpu.VMEM((2, own), jnp.int32),
            pltpu.SemaphoreType.DMA((4,)),
        ],
        FIRST_LIMIT,
    )(
        (x * CORES + core).astype(jnp.int32).reshape(1),
        expert_ids.T,
        tokens,
        shift_scale_gate,
        w_router.T,
    )
    packet = lax.all_to_all(packet, tensor, 0, 0, tiled=True)
    slots, route = call(
        fill_kernel,
        (
            jax.ShapeDtypeStruct((count, lanes), BF16),
            jax.ShapeDtypeStruct((8, members * PAD), F32),
        ),
        2 * count * members * PAD * lanes,
        4 * count * lanes,
    )(core.astype(jnp.int32).reshape(1), packet)
    arrived = lax.all_to_all(
        slots.reshape(experts, half, lanes), "expert", 0, 0, tiled=True
    ).reshape(count, lanes)

    quarter = x.astype(jnp.int32).reshape(1)
    onward = [(i, (i + 1) % chips) for i in range(chips)]
    backward = [(i, (i - 1) % chips) for i in range(chips)]
    g0, u0, w0 = weights
    g1, u1, w1 = others
    cols = gate_weight.shape[2]
    cut_rows = count // 2
    upper, lower = arrived[:cut_rows], arrived[cut_rows:]
    l0 = lax.ppermute(upper, "x", onward)
    r1 = lax.ppermute(lower, "x", backward)
    l1 = lax.ppermute(lower, "x", onward)
    r0 = lax.ppermute(upper, "x", backward)
    top = lax.ppermute(l0, "x", onward)
    bottom = lax.ppermute(r1, "x", backward)
    near = call(
        near_kernel,
        jax.ShapeDtypeStruct((4, count, cols), F32),
        24 * count * lanes * cols,
        16 * lanes * cols + 16 * count * cols,
        "vvvvvvhhhh",
        [pltpu.VMEM((4, 3, lanes, cols), BF16), pltpu.SemaphoreType.DMA((4, 3))],
    )(quarter, arrived, l0, l1, r0, r1, g0, u0, g1, u1)
    hidden, far = call(
        far_kernel,
        (
            jax.ShapeDtypeStruct((2, count, cols), BF16),
            jax.ShapeDtypeStruct((2, cut_rows, lanes), BF16),
        ),
        12 * count * lanes * cols,
        16 * count * cols,
        "vvvvhhhhhh",
        [
            pltpu.VMEM((4, lanes, cols), BF16),
            pltpu.VMEM((2, cols, lanes), BF16),
            pltpu.SemaphoreType.DMA((6,)),
        ],
    )(quarter, near, top, bottom, g0, u0, g1, u1, w0, w1)
    top = lax.ppermute(far[0], "x", onward)
    bottom = lax.ppermute(far[1], "x", backward)
    piece = jax.ShapeDtypeStruct((cut_rows, lanes), BF16)
    direct_right, direct_left = call(
        direct_kernel, (piece, piece), 4 * count * lanes * cols, 4 * count * lanes
    )(quarter, hidden, w0, w1)
    l1 = lax.ppermute(direct_right, "x", onward)
    r0 = lax.ppermute(direct_left, "x", backward)
    to_right, to_left = call(
        relay_kernel, (piece, piece), 4 * count * lanes * cols, 4 * count * lanes
    )(quarter, hidden, w0, w1, top, bottom)
    l0 = lax.ppermute(to_right, "x", onward)
    r1 = lax.ppermute(to_left, "x", backward)
    own_sum = call(
        own_kernel,
        jax.ShapeDtypeStruct((count, lanes), F32),
        4 * count * lanes * cols,
        4 * count * lanes,
    )(quarter, hidden, w0, w1)
    summed = call(
        sum_kernel,
        jax.ShapeDtypeStruct((count, lanes), BF16),
        2 * count * lanes,
        10 * count * lanes,
    )(own_sum, l0, l1, r0, r1)
    produced = lax.all_to_all(
        summed.reshape(images, half, lanes), "expert", 0, 0, tiled=True
    ).reshape(count, lanes)
    mixed = call(
        combine_kernel,
        jax.ShapeDtypeStruct((members, own, lanes), BF16),
        4 * count * members * PAD * lanes,
        4 * count * lanes,
    )(produced, route)
    mixed = lax.all_to_all(mixed, tensor, 0, 0, tiled=True)
    return call(
        gate_kernel, jax.ShapeDtypeStruct((own, width), BF16), own * width, 4 * own * width
    )(mixed, shift_scale_gate)


def solution(mesh):
    images, members = mesh.devices.shape
    fine = Mesh(mesh.devices.reshape(images, members // CORES, CORES), ("expert", "x", "c"))
    tensor = ("x", "c")
    rows = P(("expert", "x", "c"), None)
    placed = (
        rows,
        P("expert", None, None),
        P(),
        P("expert", None, tensor),
        P("expert", None, tensor),
        P("expert", tensor, None),
        rows,
    )
    return jax.shard_map(body, mesh=fine, in_specs=placed, out_specs=rows, check_vma=False)
```

```python
import functools

import jax
import jax.numpy as jnp
from jax import lax
from jax.experimental import pallas as pl
from jax.experimental.pallas import tpu as pltpu
from jax.sharding import Mesh, PartitionSpec as P

EPS = 1e-06
F32 = jnp.float32
BF16 = jnp.bfloat16
CORES = 2
SLOT = 16
PAD = 64
ROUTE = 16
VMEM_LIMIT = 12 * 1024 * 1024
FIRST_LIMIT = 60 * 1024 * 1024


def call(kernel, out_shape, flops, nbytes, spaces=None, scratch=(), limit=VMEM_LIMIT):
    kinds = {"v": pltpu.VMEM, "h": pltpu.HBM, "s": pltpu.SMEM}
    specs = {}
    if spaces is not None:
        specs = {"in_specs": [pl.BlockSpec(memory_space=kinds[kind]) for kind in spaces]}
    return pl.pallas_call(
        kernel,
        out_shape=out_shape,
        scratch_shapes=scratch,
        compiler_params=pltpu.CompilerParams(vmem_limit_bytes=limit),
        cost_estimate=pl.CostEstimate(flops=flops, bytes_accessed=nbytes, transcendentals=0),
        **specs,
    )


def high_low(value):
    high = value.astype(BF16).astype(F32)
    return high, value - high


def modulate_kernel(
    member_ref, ids_in, tokens_in, modulation_in, router_in, packet_ref,
    tokens_ref, modulation_ref, router_ref, ids_ref, arrived,
):
    copies = [
        pltpu.make_async_copy(source, target, arrived.at[index])
        for index, (source, target) in enumerate(
            (
                (tokens_in, tokens_ref),
                (modulation_in, modulation_ref),
                (router_in, router_ref),
                (ids_in, ids_ref),
            )
        )
    ]
    for copy in copies:
        copy.start()
    copies[0].wait()
    rows, width = tokens_ref.shape
    lanes = packet_ref.shape[2]
    values = tokens_ref[...].astype(F32)
    average = jnp.mean(values, axis=-1, keepdims=True)
    centred = values - average
    spread = jnp.mean(centred * centred, axis=-1, keepdims=True)
    normed = centred * lax.rsqrt(spread + EPS)
    copies[1].wait()
    copies[2].wait()
    copies[3].wait()
    modulated = (normed * (1.0 + modulation_ref[1]) + modulation_ref[0]).astype(BF16)
    logits = lax.dot_general(
        router_ref[...], modulated, (((1,), (1,)), ((), ())), preferred_element_type=F32
    )
    chance_all = jax.nn.sigmoid(logits)
    expert = lax.broadcasted_iota(jnp.int32, logits.shape, 0)
    ids = ids_ref[...]
    chance = [
        jnp.sum(jnp.where(expert == ids[c : c + 1], chance_all, 0.0), axis=0, keepdims=True)
        for c in range(2)
    ]
    total = chance[0] + chance[1]
    first_high, first_low = high_low(chance[0] / total)
    second_high, second_low = high_low(chance[1] / total)
    named = ids.astype(F32)
    route = jnp.concatenate(
        [
            named[0:1] + 1.0,
            named[1:2] + 1.0,
            first_high,
            first_low,
            second_high,
            second_low,
            jnp.zeros((ROUTE - 6, rows), F32),
        ],
        axis=0,
    ).astype(BF16)
    token = lax.broadcasted_iota(jnp.int32, (rows, lanes), 0)
    lane = lax.broadcasted_iota(jnp.int32, (rows, lanes), 1)
    place = jnp.where(lane == token + member_ref[0] * PAD, 1.0, 0.0).astype(BF16)
    placed = jnp.dot(route, place, preferred_element_type=F32).astype(BF16)
    for member in range(packet_ref.shape[0]):
        quarter = member // CORES
        packet_ref[member, 0:rows, :] = modulated[:, quarter * lanes : (quarter + 1) * lanes]
        packet_ref[member, rows:PAD, :] = placed


def fill_kernel(core_ref, packet_ref, slots_ref, route_ref):
    members, _, lanes = packet_ref.shape
    count = slots_ref.shape[0]
    half = SLOT // CORES
    experts = count // half
    tokens = PAD - ROUTE
    route = packet_ref[0, tokens:PAD, :].astype(F32)
    for member in range(1, members):
        route = route + packet_ref[member, tokens:PAD, :].astype(F32)
    everything = packet_ref.shape[0] * PAD
    named = [route[c : c + 1].astype(jnp.int32) - 1 for c in range(2)]
    expert = lax.broadcasted_iota(jnp.int32, (experts, everything), 0)
    names = [expert == named[c] for c in range(2)]
    either = jnp.where(names[0] | names[1], 1.0, 0.0).astype(BF16)
    earlier = lax.broadcasted_iota(jnp.int32, (everything, everything), 0) < (
        lax.broadcasted_iota(jnp.int32, (everything, everything), 1)
    )
    before = jnp.dot(
        either, jnp.where(earlier, 1.0, 0.0).astype(BF16), preferred_element_type=F32
    )
    place = []
    for c in range(2):
        position = jnp.sum(jnp.where(names[c], before, 0.0), axis=0, keepdims=True)
        position = position.astype(jnp.int32) - core_ref[0] * half
        here = (position >= 0) & (position < half) & (named[c] >= 0)
        place.append(jnp.where(here, named[c] * half + position, -1))
    slot = lax.broadcasted_iota(jnp.int32, (count, everything), 0)
    pick = jnp.where((slot == place[0]) | (slot == place[1]), 1.0, 0.0).astype(BF16)
    rows = packet_ref[...].reshape(everything, lanes)
    slots_ref[...] = jnp.dot(pick, rows, preferred_element_type=F32).astype(BF16)
    route_ref[...] = jnp.concatenate(
        [place[0].astype(F32), place[1].astype(F32), route[2:6], jnp.zeros((2, everything), F32)],
        axis=0,
    )


def cut(quarter_ref, step, blocks, width):
    return pl.ds(pl.multiple_of(lax.rem(quarter_ref[0] + step, blocks) * width, width), width)


def near_kernel(quarter_ref, a_ref, l0, l1, r0, r1, g0, u0, g1, u1, out_ref, held, arrived):
    rows, width = l0.shape
    blocks = g0.shape[0] // width
    copies = [
        [
            pltpu.make_async_copy(
                weight_ref.at[cut(quarter_ref, step, blocks, width), :],
                held.at[index, place],
                arrived.at[index, place],
            )
            for place, step in enumerate((0, blocks - 1, 1))
        ]
        for index, weight_ref in enumerate((g0, u0, g1, u1))
    ]
    for group in copies:
        for copy in group:
            copy.start()
    for index, group in enumerate(copies):
        for copy in group:
            copy.wait()
        for part, (l_ref, r_ref) in enumerate(((l0, r0), (l1, r1))):
            span = slice(part * rows, (part + 1) * rows)
            out_ref[index, span, :] = (
                jnp.dot(a_ref[span, :], held[index, 0], preferred_element_type=F32)
                + jnp.dot(l_ref[...], held[index, 1], preferred_element_type=F32)
                + jnp.dot(r_ref[...], held[index, 2], preferred_element_type=F32)
            )


def far_kernel(
    part, quarter_ref, near_ref, far_ref, g0, u0, g1, u1, w0, w1,
    hidden_ref, out_ref, held, held_down, arrived,
):
    rows, width = far_ref.shape
    span = slice(part * rows, (part + 1) * rows)
    blocks = g0.shape[0] // width
    where = cut(quarter_ref, blocks // 2, blocks, width)
    copies = [
        pltpu.make_async_copy(weight_ref.at[where, :], held.at[index], arrived.at[index])
        for index, weight_ref in enumerate((g0, u0, g1, u1))
    ] + [
        pltpu.make_async_copy(down_ref.at[:, where], held_down.at[core], arrived.at[4 + core])
        for core, down_ref in enumerate((w0, w1))
    ]
    for copy in copies:
        copy.start()
    for core in range(2):
        copies[2 * core].wait()
        copies[2 * core + 1].wait()
        gate, up = [
            near_ref[index, span, :]
            + jnp.dot(far_ref[...], held[index], preferred_element_type=F32)
            for index in (2 * core, 2 * core + 1)
        ]
        hidden_ref[core] = (gate * jax.nn.sigmoid(gate) * up).astype(BF16)
    copies[4].wait()
    copies[5].wait()
    out_ref[...] = (
        jnp.dot(hidden_ref[0], held_down[0], preferred_element_type=F32)
        + jnp.dot(hidden_ref[1], held_down[1], preferred_element_type=F32)
    ).astype(BF16)


def down(hidden_ref, w0, w1, where):
    return jnp.dot(hidden_ref[0], w0[:, where], preferred_element_type=F32) + jnp.dot(
        hidden_ref[1], w1[:, where], preferred_element_type=F32
    )


def direct_kernel(quarter_ref, upper_ref, lower_ref, w0, w1, right_ref, left_ref):
    rows, width = right_ref.shape
    blocks = w0.shape[1] // width
    right = down(lower_ref, w0, w1, cut(quarter_ref, 1, blocks, width))
    left = down(upper_ref, w0, w1, cut(quarter_ref, blocks - 1, blocks, width))
    right_ref[...] = right.astype(BF16)
    left_ref[...] = left.astype(BF16)


def relay_kernel(
    quarter_ref, upper_ref, lower_ref, w0, w1, top_ref, bottom_ref, right_ref, left_ref
):
    rows, width = right_ref.shape
    blocks = w0.shape[1] // width
    right = down(upper_ref, w0, w1, cut(quarter_ref, 1, blocks, width))
    left = down(lower_ref, w0, w1, cut(quarter_ref, blocks - 1, blocks, width))
    right_ref[...] = (right + top_ref[...].astype(F32)).astype(BF16)
    left_ref[...] = (left + bottom_ref[...].astype(F32)).astype(BF16)


def own_kernel(quarter_ref, upper_ref, lower_ref, w0, w1, out_ref):
    width = out_ref.shape[1]
    where = cut(quarter_ref, 0, w0.shape[1] // width, width)
    rows = upper_ref.shape[1]
    out_ref[0:rows, :] = down(upper_ref, w0, w1, where)
    out_ref[rows:, :] = down(lower_ref, w0, w1, where)


def sum_kernel(own_ref, l0, l1, r0, r1, out_ref):
    rows = l0.shape[0]
    for part, (l_ref, r_ref) in enumerate(((l0, r0), (l1, r1))):
        span = slice(part * rows, (part + 1) * rows)
        total = own_ref[span, :] + l_ref[...].astype(F32) + r_ref[...].astype(F32)
        out_ref[span, :] = total.astype(BF16)


def combine_kernel(slots_ref, route_ref, out_ref):
    count = slots_ref.shape[0]
    everything = route_ref.shape[1]
    slot = lax.broadcasted_iota(jnp.int32, (count, everything), 0)
    first = slot == route_ref[0:1].astype(jnp.int32)
    second = slot == route_ref[1:2].astype(jnp.int32)
    high = jnp.where(first, route_ref[2:3], 0.0) + jnp.where(second, route_ref[4:5], 0.0)
    low = jnp.where(first, route_ref[3:4], 0.0) + jnp.where(second, route_ref[5:6], 0.0)
    rows = slots_ref[...]
    dims = (((0,), (0,)), ((), ()))
    mixed = lax.dot_general(high.astype(BF16), rows, dims, preferred_element_type=F32)
    mixed = mixed + lax.dot_general(low.astype(BF16), rows, dims, preferred_element_type=F32)
    mixed = mixed.astype(BF16)
    tokens = out_ref.shape[1]
    for member in range(out_ref.shape[0]):
        out_ref[member] = mixed[member * PAD : member * PAD + tokens, :]


def gate_kernel(parts_ref, modulation_ref, out_ref):
    lanes = parts_ref.shape[2]
    for quarter in range(parts_ref.shape[0] // CORES):
        total = parts_ref[CORES * quarter].astype(F32)
        for core in range(1, CORES):
            total = total + parts_ref[CORES * quarter + core].astype(F32)
        cols = slice(quarter * lanes, (quarter + 1) * lanes)
        out_ref[:, cols] = (modulation_ref[2][:, cols] * total).astype(BF16)


def body(tokens, modulation, w_router, gate_weight, up_weight, down_weight, expert_ids):
    chips = lax.axis_size("x")
    members = chips * CORES
    own, width = tokens.shape
    lanes = width // chips
    experts = w_router.shape[1]
    images = lax.axis_size("expert")
    half = SLOT // CORES
    count = experts * half
    x = lax.axis_index("x")
    core = lax.axis_index("c")
    tensor = ("x", "c")
    swap = [(0, 1), (1, 0)]
    weights = [gate_weight[0], up_weight[0], down_weight[0]]
    others = [lax.ppermute(w, "c", swap) for w in weights]

    shift_scale_gate = jnp.transpose(modulation, (1, 0, 2))
    packet = call(
        modulate_kernel,
        jax.ShapeDtypeStruct((members, PAD, lanes), BF16),
        2 * own * width * experts,
        4 * own * width,
        "shhhh",
        [
            pltpu.VMEM(tokens.shape, BF16),
            pltpu.VMEM(shift_scale_gate.shape, F32),
            pltpu.VMEM((experts, width), BF16),
            pltpu.VMEM((2, own), jnp.int32),
            pltpu.SemaphoreType.DMA((4,)),
        ],
        FIRST_LIMIT,
    )(
        (x * CORES + core).astype(jnp.int32).reshape(1),
        expert_ids.T,
        tokens,
        shift_scale_gate,
        w_router.T,
    )
    packet = lax.all_to_all(packet, tensor, 0, 0, tiled=True)
    slots, route = call(
        fill_kernel,
        (
            jax.ShapeDtypeStruct((count, lanes), BF16),
            jax.ShapeDtypeStruct((8, members * PAD), F32),
        ),
        2 * count * members * PAD * lanes,
        4 * count * lanes,
    )(core.astype(jnp.int32).reshape(1), packet)
    arrived = lax.all_to_all(
        slots.reshape(experts, half, lanes), "expert", 0, 0, tiled=True
    ).reshape(count, lanes)

    quarter = x.astype(jnp.int32).reshape(1)
    onward = [(i, (i + 1) % chips) for i in range(chips)]
    backward = [(i, (i - 1) % chips) for i in range(chips)]
    g0, u0, w0 = weights
    g1, u1, w1 = others
    cols = gate_weight.shape[2]
    cut_rows = count // 2
    upper, lower = arrived[:cut_rows], arrived[cut_rows:]
    l0 = lax.ppermute(upper, "x", onward)
    r1 = lax.ppermute(lower, "x", backward)
    l1 = lax.ppermute(lower, "x", onward)
    r0 = lax.ppermute(upper, "x", backward)
    top = lax.ppermute(l0, "x", onward)
    bottom = lax.ppermute(r1, "x", backward)
    near = call(
        near_kernel,
        jax.ShapeDtypeStruct((4, count, cols), F32),
        24 * count * lanes * cols,
        16 * lanes * cols + 16 * count * cols,
        "vvvvvvhhhh",
        [pltpu.VMEM((4, 3, lanes, cols), BF16), pltpu.SemaphoreType.DMA((4, 3))],
    )(quarter, arrived, l0, l1, r0, r1, g0, u0, g1, u1)
    halves = []
    for part, came in ((1, bottom), (0, top)):
        halves.append(
            call(
                functools.partial(far_kernel, part),
                (
                    jax.ShapeDtypeStruct((2, cut_rows, cols), BF16),
                    jax.ShapeDtypeStruct((cut_rows, lanes), BF16),
                ),
                6 * count * lanes * cols,
                8 * count * cols,
                "vvvhhhhhh",
                [
                    pltpu.VMEM((4, lanes, cols), BF16),
                    pltpu.VMEM((2, cols, lanes), BF16),
                    pltpu.SemaphoreType.DMA((6,)),
                ],
            )(quarter, near, came, g0, u0, g1, u1, w0, w1)
        )
    (lower_hidden, lower_far), (upper_hidden, upper_far) = halves
    bottom = lax.ppermute(lower_far, "x", backward)
    top = lax.ppermute(upper_far, "x", onward)
    piece = jax.ShapeDtypeStruct((cut_rows, lanes), BF16)
    direct_right, direct_left = call(
        direct_kernel, (piece, piece), 4 * count * lanes * cols, 4 * count * lanes
    )(quarter, upper_hidden, lower_hidden, w0, w1)
    l1 = lax.ppermute(direct_right, "x", onward)
    r0 = lax.ppermute(direct_left, "x", backward)
    to_right, to_left = call(
        relay_kernel, (piece, piece), 4 * count * lanes * cols, 4 * count * lanes
    )(quarter, upper_hidden, lower_hidden, w0, w1, top, bottom)
    l0 = lax.ppermute(to_right, "x", onward)
    r1 = lax.ppermute(to_left, "x", backward)
    own_sum = call(
        own_kernel,
        jax.ShapeDtypeStruct((count, lanes), F32),
        4 * count * lanes * cols,
        4 * count * lanes,
    )(quarter, upper_hidden, lower_hidden, w0, w1)
    summed = call(
        sum_kernel,
        jax.ShapeDtypeStruct((count, lanes), BF16),
        2 * count * lanes,
        10 * count * lanes,
    )(own_sum, l0, l1, r0, r1)
    produced = lax.all_to_all(
        summed.reshape(images, half, lanes), "expert", 0, 0, tiled=True
    ).reshape(count, lanes)
    mixed = call(
        combine_kernel,
        jax.ShapeDtypeStruct((members, own, lanes), BF16),
        4 * count * members * PAD * lanes,
        4 * count * lanes,
    )(produced, route)
    mixed = lax.all_to_all(mixed, tensor, 0, 0, tiled=True)
    return call(
        gate_kernel, jax.ShapeDtypeStruct((own, width), BF16), own * width, 4 * own * width
    )(mixed, shift_scale_gate)


def solution(mesh):
    images, members = mesh.devices.shape
    fine = Mesh(mesh.devices.reshape(images, members // CORES, CORES), ("expert", "x", "c"))
    tensor = ("x", "c")
    rows = P(("expert", "x", "c"), None)
    placed = (
        rows,
        P("expert", None, None),
        P(),
        P("expert", None, tensor),
        P("expert", None, tensor),
        P("expert", tensor, None),
        rows,
    )
    return jax.shard_map(body, mesh=fine, in_specs=placed, out_specs=rows, check_vma=False)
```
